32 devices in a mesh: row: 8 (over z, core), col: 2 (over x), depth: 2 (over y).
Axes of the slice: x: 2, y: 2, z: 4, core: 2. Of those that a mesh axis runs over, the one named last changes fastest.
Arguments:
- a_blocks: float32 [16, 16, 256, 256], P('row', ('depth', 'col')), may hold values from -6 to 6
- a_pattern: int32 [16, 16], P('row', ('depth', 'col')), may hold values from 0 to 1, as said below
- b_blocks: float32 [16, 8, 256, 256], P(('depth', 'row'), 'col'), may hold values from -0.1875 to 0.1875
- b_pattern: int32 [16, 8], P(('depth', 'row'), 'col'), may hold values from 0 to 1, as said below
- c_pattern: int32 [16, 8], P(('row', 'depth'), 'col'), may hold values 0 or 1
Outputs:
- c_blocks: float32 [16, 8, 256, 256], P(('row', 'depth'), 'col')
The draws below stay inside these ranges and needn't reach their ends.
Inputs may be any that keep to these rules, and one draw needn't show every extreme that they name: Each block row of a_pattern holds between 1 and 4 stored blocks, and some block row holds exactly 4. Each block column of b_pattern holds between 1 and 4 stored blocks, and some block column holds exactly 4.
All inputs are finite; a program needn't handle non-finite values. No bound on the sum of `c_pattern` on one device may be relied on, other than what follows from the above.
Results may differ from the reference program's by a relative error of at most 0.000071.
Values sent between devices are 32-bit elements; how exact they have to be, the bound alone decides.
No kernel may reach another device: no remote copies, remote signals or barrier semaphores. Data moves between devices by JAX's collectives and lax.ppermute only.
A program may use at most 128 MiB of HBM per device.

```python
import jax
import jax.numpy as jnp
from jax import lax

BS = 256
NR = 16
NC = 8
NK = 16


def limited_rows(key, rows, cols, most):
    first, second, third = jax.random.split(key, 3)
    scores = jax.random.randint(first, (rows, cols), 0, 1 << 20) * cols + jnp.arange(cols, dtype=jnp.int32)[None, :]
    ranks = jnp.argsort(jnp.argsort(scores, axis=1), axis=1)
    counts = jax.random.randint(second, (rows,), 1, most + 1)
    chosen = jax.random.randint(third, (), 0, rows)
    counts = jnp.where(jnp.arange(rows) == chosen, most, counts)
    return (ranks < counts[:, None]).astype(jnp.int32)


def draw_a_pattern(key, part):
    return limited_rows(jax.random.fold_in(key, 11), NR, NK, NK // 4)


def draw_b_pattern(key, part):
    return limited_rows(jax.random.fold_in(key, 23), NC, NK, NK // 4).T


def with_ends(entries, key, least, high):
    spot = [jax.random.randint(jax.random.fold_in(key, axis), (), 0, length) for axis, length in enumerate(entries.shape)]
    longest = entries.shape.index(max(entries.shape))
    beside = spot[:longest] + [(spot[longest] + 1) % entries.shape[longest]] + spot[longest + 1:]
    return entries.at[tuple(spot)].set(least).at[tuple(beside)].set(high)


def shard_levels(rng, shape, pieces, smallest, top_value):
    loudness, own = 1.0, jax.random.fold_in(rng, 6)
    for position, parts in pieces:
        draws = jnp.exp(jax.random.uniform(jax.random.fold_in(own, position), (parts,), jnp.float32, smallest / len(pieces), top_value / len(pieces)))
        loudness = loudness * jnp.repeat(draws, shape[position] // parts).reshape([-1 if axis == position else 1 for axis in range(len(shape))])
    return loudness


def bell_draw(own_key, dims, spread, most, cuts=(), kind=jnp.bfloat16):
    values = jax.random.normal(own_key, dims, jnp.float32) * spread
    if len(cuts) > 0:
        values = shard_levels(own_key, dims, cuts, -0.22, 0.18) * values
    return jnp.clip(values, min=-most, max=most).astype(kind)


def setup_inputs(seed: int = 0) -> dict:
    key_list = jax.random.split(jax.random.key(seed), 6)
    a_blocks = bell_draw(key_list[0], (NR, NK, BS, BS), 1.0, 6.0, ((0, 8), (1, 4)), jnp.float32)
    a_pattern = draw_a_pattern(jax.random.fold_in(key_list[5], 71), 0)
    b_blocks = bell_draw(key_list[2], (NK, NC, BS, BS), (NK * BS // 4) ** -0.5, 0.1875, ((0, 16), (1, 2)), jnp.float32)
    b_pattern = draw_b_pattern(jax.random.fold_in(key_list[5], 71), 0)
    c_pattern = with_ends((jax.random.randint(key_list[4], (NR, NC), 0, 2) < 1).astype(jnp.int32), jax.random.fold_in(key_list[4], 1), 0, 1)
    return {"a_blocks": a_blocks, "a_pattern": a_pattern, "b_blocks": b_blocks, "b_pattern": b_pattern, "c_pattern": c_pattern}


def reference(a_blocks, a_pattern, b_blocks, b_pattern, c_pattern):
    left = a_blocks * a_pattern[:, :, None, None].astype(jnp.float32)
    right = b_blocks * b_pattern[:, :, None, None].astype(jnp.float32)
    product = jnp.einsum("rkab,kcbe->rcae", left, right, precision=lax.Precision.HIGHEST)
    return product * c_pattern[:, :, None, None].astype(jnp.float32)
```

```python
import functools

import jax
import jax.numpy as jnp
import numpy as np
from jax import lax
from jax.experimental import pallas as pl
from jax.experimental.pallas import tpu as pltpu
from jax.sharding import PartitionSpec as P

LANES = 128
F32 = jnp.float32
SMEM = pl.BlockSpec(memory_space=pltpu.SMEM)
VMEM = pl.BlockSpec(memory_space=pltpu.VMEM)
ANY = pl.BlockSpec(memory_space=pl.ANY)
PARAMS = pltpu.CompilerParams(vmem_limit_bytes=48 * 1024 * 1024)


class Plan:
    def __init__(self, mesh, a_blocks, b_blocks):
        self.nrow, self.ncol, self.ndep = (mesh.shape[name] for name in ("row", "col", "depth"))
        self.rows, self.kc, self.bs, _ = a_blocks.shape
        self.kb, self.nc, _, _ = b_blocks.shape
        assert self.kb == 1 and self.rows == self.ndep
        every = self.nrow * self.ncol * self.ndep
        self.whole = self.bs // every >= 8
        self.axes = ("row", "col", "depth") if self.whole else ("row", "depth")
        self.G = every if self.whole else self.nrow * self.ndep
        self.R = self.bs // self.G
        self.Q = self.G * self.nc
        self.W = self.kc if self.whole else self.kc * self.ncol
        self.nk = self.kc * self.ncol * self.ndep
        self.most = self.nc * (self.nk // 4)
        self.levels = sorted({min(level, self.most) for level in (2, 3, 4, 5, 6, self.most)})

    def decode(self, s):
        if self.whole:
            return s // (self.ncol * self.ndep), s // self.ndep % self.ncol, s % self.ndep
        return s // self.ndep, s * 0, s % self.ndep

    def tables(self):
        q = np.arange(self.Q)[None, :]
        s = np.arange(self.G)[:, None]
        e = np.arange(LANES)[:, None]
        row_q, col_q, dep_q = self.decode(q % self.G)
        c_q = q // self.G
        row_s, col_s, dep_s = self.decode(s)
        row_t, col_t, dep_t = self.decode(s.T)
        kk = row_q % self.W
        select = [e == rr * self.W + kk for rr in range(self.rows)]
        select += [e == self.rows * self.W + c_q, e == self.rows * self.W + self.nc + c_q]
        holds = (dep_s == dep_q) & (col_s == row_q // self.W)
        own = s == q % self.G
        same_col = col_s == col_q
        before = np.arange(self.Q)[:, None] < q
        pick = [(row_s == row_t) & (dep_s == rr) for rr in range(self.rows)]
        wide = np.concatenate(select, axis=1)
        masks = np.concatenate([holds, own, same_col], axis=0)
        return [jnp.asarray(t.astype(np.float32)) for t in (wide, masks, before, np.concatenate(pick, axis=1))]


def prepare(plan, ap, bp, cp, b_ref, out_ref):
    wide = plan.nc * plan.bs
    for c in range(plan.nc):
        out_ref[:, :, c * plan.bs : (c + 1) * plan.bs] = b_ref[0, c].reshape(plan.G, plan.R, plan.bs)
    lane = lax.broadcasted_iota(jnp.int32, (plan.R, LANES), 1)
    entries = [ap[r, k] for r in range(plan.rows) for k in range(plan.W)]
    entries += [bp[0, c] for c in range(plan.nc)] + [cp[0, c] for c in range(plan.nc)]
    tile = jnp.zeros((plan.R, LANES), F32)
    for place, value in enumerate(entries):
        tile = jnp.where(lane == place, value.astype(F32), tile)
    for s in range(plan.G):
        out_ref[s, :, wide : wide + LANES] = tile


def dot(x, y):
    return jnp.dot(x, y, preferred_element_type=F32)


def schedule(plan, p_ref, wide, masks, before, pick, table_ref, most_ref):
    G, Q = plan.G, plan.Q
    entries = dot(p_ref[:, 0, plan.nc * plan.bs :], wide[...])
    holds, own, same_col = masks[0:G], masks[G : 2 * G], masks[2 * G : 3 * G]
    stored_a = jnp.zeros((G, Q), F32)
    for rr in range(plan.rows):
        stored_a += dot(pick[:, rr * G : (rr + 1) * G], entries[:, rr * Q : (rr + 1) * Q] * holds)
    stored_b = jnp.sum(entries[:, plan.rows * Q : (plan.rows + 1) * Q] * own, axis=0, keepdims=True)
    need = stored_a * stored_b * entries[:, (plan.rows + 1) * Q :] * same_col
    rank = dot(need, before[...])
    count = jnp.sum(need, axis=1, keepdims=True)
    q = lax.broadcasted_iota(jnp.int32, (G, Q), 1).astype(F32)
    lane = lax.broadcasted_iota(jnp.int32, (G, LANES), 1)
    table = jnp.where(lane == LANES - 1, count, 0.0)
    for j in range(plan.most):
        at = jnp.sum(jnp.where(rank == float(j), need, 0.0) * q, axis=1, keepdims=True)
        table = jnp.where(lane == j, at, table)
    table_ref[...] = table.astype(jnp.int32)
    most_ref[0] = jnp.max(count).astype(jnp.int32)


def pack(plan, J, table, got_ref, out_ref):
    def body(d, carry):
        for j in range(J):
            q = table[d, j]
            start = pl.multiple_of(q // plan.G * plan.bs, plan.bs)
            out_ref[d, j] = got_ref[q % plan.G, :, pl.ds(start, plan.bs)]
        return carry

    lax.fori_loop(0, plan.G, body, 0)


def multiply(plan, J, me, table, got_ref, *refs):
    lefts, out_ref, a_scr, sems = refs[:-3], refs[-3], refs[-2], refs[-1]
    member, col, dep = me[0], me[1], me[2]
    count = table[member, LANES - 1]

    def place(j):
        q = table[member, j]
        row_s, _, dep_s = plan.decode(q % plan.G)
        dd = (dep - dep_s + plan.ndep) % plan.ndep
        dc = (col - row_s // plan.kc + plan.ncol) % plan.ncol
        return dd * plan.ncol + dc, row_s % plan.kc, q // plan.G

    for j in range(J):
        which, kk, _ = place(j)
        for n, left in enumerate(lefts):

            @pl.when((j < count) & (which == n))
            def _(left=left, n=n):
                src = left.at[dep, kk] if n == 0 else left.at[kk]
                pltpu.make_async_copy(src, a_scr.at[j], sems.at[j]).start()

    out_ref[...] = jnp.zeros_like(out_ref)
    for j in range(J):

        @pl.when(j < count)
        def _():
            pltpu.make_async_copy(lefts[1].at[0], a_scr.at[j], sems.at[j]).wait()
            _, _, c = place(j)
            right = got_ref[:, j].reshape(plan.bs, plan.bs)
            out_ref[0, c] += jnp.dot(a_scr[j], right, precision=lax.Precision.HIGHEST, preferred_element_type=F32)


def local(mesh, a_blocks, a_pattern, b_blocks, b_pattern, c_pattern):
    plan = Plan(mesh, a_blocks, b_blocks)
    G, R, bs, nc = plan.G, plan.R, plan.bs, plan.nc
    col, dep = lax.axis_index("col"), lax.axis_index("depth")
    me = jnp.stack([lax.axis_index(plan.axes), col, dep]).astype(jnp.int32)

    lefts = [a_blocks]
    for dd in range(plan.ndep):
        send = lax.dynamic_index_in_dim(a_blocks, (dep + dd) % plan.ndep, axis=0, keepdims=False)
        for dc in range(plan.ncol):
            if (dd, dc) != (0, 0):
                perm = [
                    (x * plan.ndep + y, (x + dc) % plan.ncol * plan.ndep + (y + dd) % plan.ndep)
                    for x in range(plan.ncol)
                    for y in range(plan.ndep)
                ]
                lefts.append(lax.ppermute(send, ("col", "depth"), perm))

    if not plan.whole:
        a_pattern = lax.all_gather(a_pattern, "col", axis=1, tiled=True)
    pieces = pl.pallas_call(
        functools.partial(prepare, plan),
        out_shape=jax.ShapeDtypeStruct((G, R, nc * bs + LANES), F32),
        in_specs=[SMEM, SMEM, SMEM, VMEM],
        out_specs=VMEM,
        compiler_params=PARAMS,
        name="prepare",
    )(a_pattern, b_pattern, c_pattern, b_blocks)
    got = lax.all_to_all(pieces, plan.axes, 0, 0, tiled=True)
    table, most = pl.pallas_call(
        functools.partial(schedule, plan),
        out_shape=(jax.ShapeDtypeStruct((G, LANES), jnp.int32), jax.ShapeDtypeStruct((1,), jnp.int32)),
        in_specs=[VMEM] * 5,
        out_specs=(VMEM, SMEM),
        compiler_params=PARAMS,
        name="schedule",
    )(got, *plan.tables())
    most = most[0]
    if not plan.whole:
        most = lax.pmax(most, "col")

    def branch(J, got, table, me, *lefts):
        send = pl.pallas_call(
            functools.partial(pack, plan, J),
            out_shape=jax.ShapeDtypeStruct((G, J, R, bs), F32),
            in_specs=[SMEM, VMEM],
            out_specs=VMEM,
            compiler_params=PARAMS,
            name="pack",
        )(table, got)
        blocks = lax.all_to_all(send, plan.axes, 0, 0, tiled=True)
        return pl.pallas_call(
            functools.partial(multiply, plan, J),
            out_shape=jax.ShapeDtypeStruct((1, nc, bs, bs), F32),
            in_specs=[SMEM, SMEM, VMEM] + [ANY] * len(lefts),
            out_specs=VMEM,
            scratch_shapes=[pltpu.VMEM((J, bs, bs), F32), pltpu.SemaphoreType.DMA((J,))],
            compiler_params=PARAMS,
            name="multiply",
        )(me, table, blocks, *lefts)

    index = sum((most > level).astype(jnp.int32) for level in plan.levels[:-1])
    return lax.switch(index, [functools.partial(branch, level) for level in plan.levels], got, table, me, *lefts)


def solution(mesh):
    in_specs = (
        P("row", ("depth", "col"), None, None),
        P("row", ("depth", "col")),
        P(("depth", "row"), "col", None, None),
        P(("depth", "row"), "col"),
        P(("row", "depth"), "col"),
    )
    out_specs = P(("row", "depth"), "col", None, None)
    return jax.shard_map(
        functools.partial(local, mesh), mesh=mesh, in_specs=in_specs, out_specs=out_specs, check_vma=False
    )
```

```python
import functools

import jax
import jax.numpy as jnp
import numpy as np
from jax import lax
from jax.experimental import pallas as pl
from jax.experimental.pallas import tpu as pltpu
from jax.sharding import PartitionSpec as P

LANES = 128
F32 = jnp.float32
I32 = jnp.int32
SMEM = pl.BlockSpec(memory_space=pltpu.SMEM)
VMEM = pl.BlockSpec(memory_space=pltpu.VMEM)
HBM = pl.BlockSpec(memory_space=pltpu.HBM)
PARAMS = pltpu.CompilerParams(vmem_limit_bytes=48 * 1024 * 1024)


class Plan:
    def __init__(self, mesh, a_blocks, b_blocks):
        self.nrow, self.ncol, self.ndep = (mesh.shape[name] for name in ("row", "col", "depth"))
        self.rows, self.kc, self.bs, _ = a_blocks.shape
        self.kb, self.nc, _, _ = b_blocks.shape
        assert self.kb == 1 and self.rows == self.ndep
        every = self.nrow * self.ncol * self.ndep
        self.whole = self.bs // every >= 8
        self.axes = ("row", "col", "depth") if self.whole else ("row", "depth")
        self.G = every if self.whole else self.nrow * self.ndep
        self.R = self.bs // self.G
        self.Q = self.G * self.nc
        self.W = self.kc if self.whole else self.kc * self.ncol
        self.nk = self.kc * self.ncol * self.ndep
        self.most = self.nc * (self.nk // 4)
        self.slots = min(3, self.nc)
        self.others = [(dd, dc) for dd in range(self.ndep) for dc in range(self.ncol) if (dd, dc) != (0, 0)]
        few = min(2, self.kc)
        steps = sorted({min(level, self.most) for level in (2, 3, 4, 5, 6)})
        self.levels = [(step, few, False) for step in steps]
        self.levels += [(steps[-1], self.kc, False), (steps[-1], self.kc, True), (self.most, self.kc, True)]

    def decode(self, s):
        if self.whole:
            return s // (self.ncol * self.ndep), s // self.ndep % self.ncol, s % self.ndep
        return s // self.ndep, s * 0, s % self.ndep

    def tables(self):
        q = np.arange(self.Q)[None, :]
        s = np.arange(self.G)[:, None]
        e = np.arange(LANES)[:, None]
        row_q, col_q, dep_q = self.decode(q % self.G)
        c_q = q // self.G
        row_s, col_s, dep_s = self.decode(s)
        row_t, _, dep_t = self.decode(s.T)
        b0 = self.rows * self.W
        select = [e == rr * self.W + row_q % self.W for rr in range(self.rows)]
        select += [e == b0 + c_q, e == b0 + self.nc + c_q, (e >= b0) & (e < b0 + c_q)]
        holds = (dep_s == dep_q) & (col_s == row_q // self.W)
        masks = [holds, s == q % self.G, col_s == col_q]
        before = np.arange(self.Q)[:, None] < q
        k = np.arange(LANES)[None, :]
        inner = (dep_q * self.nrow + row_q).T == k
        chunk = (k.T < k) & (k.T // self.kc == k // self.kc) & (k < self.nk)
        far = s * 0 + k // self.kc != dep_s * self.ncol + col_s
        pick = [(row_s == row_t) & (dep_s == rr) for rr in range(self.rows)]
        groups = [np.concatenate(select, 1), np.concatenate(masks, 0), np.concatenate([before, inner], 1)]
        groups += [np.concatenate([chunk, far], 0), np.concatenate(pick, 1)]
        return [jnp.asarray(t.astype(np.float32)) for t in groups]


def prepare(plan, ap_hbm, bp_hbm, cp_hbm, b_hbm, out_hbm, ap, bp, cp, tile_ref, sems, block_sems):
    copies = [(bp_hbm, bp), (ap_hbm, ap), (cp_hbm, cp)]
    copies = [pltpu.make_async_copy(src, dst, sems.at[n]) for n, (src, dst) in enumerate(copies)]
    for copy in copies:
        copy.start()
    copies[0].wait()

    def piece(c, j):
        return pltpu.make_async_copy(b_hbm.at[c], out_hbm.at[:, :, pl.ds(j * plan.bs, plan.bs)], block_sems.at[j])

    count = jnp.int32(0)
    for c in range(plan.nc):
        stored = bp[0, c] != 0
        for j in range(plan.slots):

            @pl.when(stored & (count == j))
            def _(c=c, j=j):
                piece(c, j).start()

        count += stored.astype(I32)

    for copy in copies[1:]:
        copy.wait()
    lane = lax.broadcasted_iota(I32, (plan.R, LANES), 1)
    entries = [ap[r, k] for r in range(plan.rows) for k in range(plan.W)]
    entries += [bp[0, c] for c in range(plan.nc)] + [cp[0, c] for c in range(plan.nc)]
    tile = jnp.zeros((plan.R, LANES), F32)
    for place, value in enumerate(entries):
        tile = jnp.where(lane == place, value.astype(F32), tile)
    tile_ref[...] = jnp.broadcast_to(tile[None], tile_ref.shape)
    last = pltpu.make_async_copy(tile_ref, out_hbm.at[:, :, pl.ds(plan.slots * plan.bs, LANES)], sems.at[3])
    last.start()
    for j in range(plan.slots):

        @pl.when(count > j)
        def _(j=j):
            piece(0, j).wait()

    last.wait()


def dot(x, y):
    return jnp.dot(x, y, preferred_element_type=F32)


def schedule(plan, p_ref, wide, masks, after, chunk, pick, table_ref, left_ref, index_ref):
    G, Q, nk = plan.G, plan.Q, plan.nk
    entries = dot(p_ref[:, 0, :], wide[...])
    holds, own, same_col = masks[0:G], masks[G : 2 * G], masks[2 * G : 3 * G]
    stored_a = jnp.zeros((G, Q), F32)
    for rr in range(plan.rows):
        stored_a += dot(pick[:, rr * G : (rr + 1) * G], entries[:, rr * Q : (rr + 1) * Q] * holds)
    b0 = plan.rows * Q
    stored_b = jnp.sum(entries[:, b0 : b0 + Q] * own, axis=0, keepdims=True)
    slot = jnp.sum(entries[:, b0 + 2 * Q : b0 + 3 * Q] * own, axis=0, keepdims=True)
    need = stored_a * stored_b * entries[:, b0 + Q : b0 + 2 * Q] * same_col
    ranks = dot(need, after[...])
    rank = ranks[:, :Q]
    left = jnp.minimum(ranks[:, Q:], 1.0)
    place = dot(left, chunk[0:LANES])
    count = jnp.sum(need, axis=1, keepdims=True)
    name = slot * float(Q) + lax.broadcasted_iota(I32, (1, Q), 1).astype(F32)
    lane = lax.broadcasted_iota(I32, (G, LANES), 1)
    table = jnp.where(lane == LANES - 1, count, 0.0)
    for j in range(plan.most):
        at = jnp.sum(jnp.where(rank == float(j), need, 0.0) * name, axis=1, keepdims=True)
        table = jnp.where(lane == j, at, table)
    table_ref[...] = table.astype(I32)
    left_ref[...] = jnp.where(left > 0, place, -1.0).astype(I32)

    most = jnp.max(count)
    spread = jnp.max(need * slot) + 1.0
    if plan.whole:
        lefts = jnp.max(left * chunk[LANES:] * (place + 1.0))
    else:
        lefts = jnp.float32(0)
    index = jnp.int32(len(plan.levels) - 1)
    for n in reversed(range(len(plan.levels) - 1)):
        step, few, again = plan.levels[n]
        fits = (most <= step) & (lefts <= few)
        if not again:
            fits = fits & (spread <= plan.slots)
        index = jnp.where(fits, n, index)
    index_ref[0] = index


def pack(plan, J, few, again, table, left, got_ref, a_hbm, out_ref, *refs):
    outs, sems = refs[:-1], refs[-1]
    row, col, dep = lax.axis_index("row"), lax.axis_index("col"), lax.axis_index("depth")

    def each(act):
        for o, out in enumerate(outs):
            dd, dc = plan.others[o]
            to_dep, to_col = (dep + dd) % plan.ndep, (col + dc) % plan.ncol
            member = (row * plan.ncol + to_col) * plan.ndep + to_dep
            for kk in range(plan.kc):
                place = left[member, dep * plan.nrow + col * plan.kc + kk]

                @pl.when((place >= 0) & (place < few))
                def _():
                    at = jnp.clip(place, 0, few - 1)
                    act(pltpu.make_async_copy(a_hbm.at[to_dep, kk], out.at[at], sems.at[o, kk]))

    each(lambda copy: copy.start())

    def body(d, carry):
        for j in range(J):
            q = table[d, j]
            place = q // plan.G % plan.nc if again else q // plan.Q
            start = pl.multiple_of(place * plan.bs, plan.bs)
            out_ref[d, j] = got_ref[q % plan.G, :, pl.ds(start, plan.bs)]
        return carry

    lax.fori_loop(0, plan.G, body, 0)
    each(lambda copy: copy.wait())


def multiply(plan, J, table, left, got_ref, a_hbm, *refs):
    lefts, (out_hbm, a_scr, out_scr, sems, out_sems) = refs[:-5], refs[-5:]
    col, dep = lax.axis_index("col"), lax.axis_index("depth")
    member = lax.axis_index(plan.axes)
    count = table[member, LANES - 1]

    def place(j):
        q = table[member, j]
        row_s, _, dep_s = plan.decode(q % plan.G)
        return row_s, dep_s, q // plan.G % plan.nc

    def copy(src, j):
        return pltpu.make_async_copy(src, a_scr.at[j], sems.at[j])

    for j in range(J):
        row_s, dep_s, _ = place(j)
        dd = (dep - dep_s + plan.ndep) % plan.ndep
        dc = (col - row_s // plan.kc + plan.ncol) % plan.ncol
        kk = row_s % plan.kc
        for n, (xd, xc) in enumerate([(0, 0)] + plan.others):

            @pl.when((j < count) & (dd == xd) & (dc == xc))
            def _(n=n):
                if n == 0:
                    copy(a_hbm.at[dep, kk], j).start()
                else:
                    src = lefts[n - 1]
                    at = left[member, dep_s * plan.nrow + row_s] if plan.whole else kk
                    copy(src.at[jnp.clip(at, 0, src.shape[0] - 1)], j).start()

    out_scr[...] = jnp.zeros_like(out_scr)
    for j in range(J):

        @pl.when(j < count)
        def _():
            copy(a_hbm.at[0, 0], j).wait()
            _, _, c = place(j)
            right = got_ref[:, j].reshape(plan.bs, plan.bs)
            out_scr[c] += jnp.dot(a_scr[j], right, precision=lax.Precision.HIGHEST, preferred_element_type=F32)

    whole = pltpu.make_async_copy(out_scr, out_hbm.at[0], out_sems.at[0])
    whole.start()
    whole.wait()


def local(mesh, a_blocks, a_pattern, b_blocks, b_pattern, c_pattern):
    plan = Plan(mesh, a_blocks, b_blocks)
    G, R, bs, nc, slots = plan.G, plan.R, plan.bs, plan.nc, plan.slots
    DMA = pltpu.SemaphoreType.DMA

    def call(kernel, out_shape, in_specs, out_specs, scratch=(), **kwargs):
        name = kernel.func.__name__
        return pl.pallas_call(
            kernel,
            out_shape=out_shape,
            in_specs=in_specs,
            out_specs=out_specs,
            scratch_shapes=scratch,
            compiler_params=PARAMS,
            name=name,
            **kwargs,
        )

    def shift(value, dd, dc):
        perm = [
            (x * plan.ndep + y, (x + dc) % plan.ncol * plan.ndep + (y + dd) % plan.ndep)
            for x in range(plan.ncol)
            for y in range(plan.ndep)
        ]
        return lax.ppermute(value, ("col", "depth"), perm)

    raw_lefts = []
    if not plan.whole:
        a_pattern = lax.all_gather(a_pattern, "col", axis=1, tiled=True)
        dep = lax.axis_index("depth")
        for dd, dc in plan.others:
            send = lax.dynamic_index_in_dim(a_blocks, (dep + dd) % plan.ndep, axis=0, keepdims=False)
            raw_lefts.append(shift(send, dd, dc))

    b_pieces = b_blocks.reshape(nc, G, R, bs)
    pieces = call(
        functools.partial(prepare, plan),
        jax.ShapeDtypeStruct((G, R, slots * bs + LANES), F32),
        [HBM, HBM, HBM, HBM],
        HBM,
        [
            pltpu.SMEM(a_pattern.shape, I32),
            pltpu.SMEM(b_pattern.shape, I32),
            pltpu.SMEM(c_pattern.shape, I32),
            pltpu.VMEM((G, R, LANES), F32),
            DMA((4,)),
            DMA((slots,)),
        ],
    )(a_pattern, b_pattern, c_pattern, b_pieces)
    got = lax.all_to_all(pieces, plan.axes, 0, 0, tiled=True)
    tables = plan.tables()
    table, left, index = call(
        functools.partial(schedule, plan),
        (
            jax.ShapeDtypeStruct((G, LANES), I32),
            jax.ShapeDtypeStruct((G, LANES), I32),
            jax.ShapeDtypeStruct((1,), I32),
        ),
        [pl.BlockSpec((G, R, LANES), lambda i: (0, 0, slots * bs // LANES))]
        + [pl.BlockSpec(t.shape, lambda i: (0, 0)) for t in tables],
        (VMEM, VMEM, SMEM),
        grid=(1,),
    )(got, *tables)
    index = index[0]
    if not plan.whole:
        index = lax.pmax(index, "col")

    def branch(J, few, again, got, table, left, a_blocks, b_pieces, *lefts):
        if again:
            got = lax.all_to_all(b_pieces.transpose(1, 2, 0, 3).reshape(G, R, nc * bs), plan.axes, 0, 0, tiled=True)
        sends = len(plan.others) if plan.whole else 0
        send, *chosen = call(
            functools.partial(pack, plan, J, few, again),
            (jax.ShapeDtypeStruct((G, J, R, bs), F32),) + (jax.ShapeDtypeStruct((few, bs, bs), F32),) * sends,
            [SMEM, SMEM, VMEM, HBM],
            (VMEM,) + (HBM,) * sends,
            [DMA((len(plan.others), plan.kc))],
        )(table, left, got, a_blocks)
        if plan.whole:
            lefts = [shift(x, dd, dc) for x, (dd, dc) in zip(chosen, plan.others)]
        blocks = lax.all_to_all(send, plan.axes, 0, 0, tiled=True)
        return call(
            functools.partial(multiply, plan, J),
            jax.ShapeDtypeStruct((1, nc, bs, bs), F32),
            [SMEM, SMEM, VMEM] + [HBM] * (1 + len(lefts)),
            HBM,
            [pltpu.VMEM((J, bs, bs), F32), pltpu.VMEM((nc, bs, bs), F32), DMA((J,)), DMA((1,))],
        )(table, left, blocks, a_blocks, *lefts)

    branches = [functools.partial(branch, *level) for level in plan.levels]
    return lax.switch(index, branches, got, table, left, a_blocks, b_pieces, *raw_lefts)


def solution(mesh):
    in_specs = (
        P("row", ("depth", "col"), None, None),
        P("row", ("depth", "col")),
        P(("depth", "row"), "col", None, None),
        P(("depth", "row"), "col"),
        P(("row", "depth"), "col"),
    )
    out_specs = P(("row", "depth"), "col", None, None)
    return jax.shard_map(
        functools.partial(local, mesh), mesh=mesh, in_specs=in_specs, out_specs=out_specs, check_vma=False
    )
```

```python
import functools

import jax
import jax.numpy as jnp
import numpy as np
from jax import lax
from jax.experimental import pallas as pl
from jax.experimental.pallas import tpu as pltpu
from jax.sharding import PartitionSpec as P

LANES = 128
F32 = jnp.float32
I32 = jnp.int32
SMEM = pl.BlockSpec(memory_space=pltpu.SMEM)
VMEM = pl.BlockSpec(memory_space=pltpu.VMEM)
HBM = pl.BlockSpec(memory_space=pltpu.HBM)
PARAMS = pltpu.CompilerParams(vmem_limit_bytes=48 * 1024 * 1024)


class Plan:
    def __init__(self, mesh, a_blocks, b_blocks):
        self.nrow, self.ncol, self.ndep = (mesh.shape[name] for name in ("row", "col", "depth"))
        self.rows, self.kc, self.bs, _ = a_blocks.shape
        self.kb, self.nc, _, _ = b_blocks.shape
        assert self.kb == 1 and self.rows == self.ndep
        every = self.nrow * self.ncol * self.ndep
        self.whole = self.bs // every >= 8
        self.axes = ("row", "col", "depth") if self.whole else ("row", "depth")
        self.G = every if self.whole else self.nrow * self.ndep
        self.R = self.bs // self.G
        self.Q = self.G * self.nc
        self.W = self.kc if self.whole else self.kc * self.ncol
        self.nk = self.kc * self.ncol * self.ndep
        self.most = self.nc * (self.nk // 4)
        self.slots = min(3, self.nc)
        self.others = [(dd, dc) for dd in range(self.ndep) for dc in range(self.ncol) if (dd, dc) != (0, 0)]
        self.early = min(2, self.kc)
        self.levels = [(step, 0, False) for step in (2, 3, 4, 5, 6)]
        self.levels += [(step, 1, False) for step in (3, 4, 6)]
        self.levels += [(6, self.kc, True), (self.most, self.kc, True)]

    def decode(self, s):
        if self.whole:
            return s // (self.ncol * self.ndep), s // self.ndep % self.ncol, s % self.ndep
        return s // self.ndep, s * 0, s % self.ndep

    def tables(self):
        q = np.arange(self.Q)[None, :]
        s = np.arange(self.G)[:, None]
        e = np.arange(LANES)[:, None]
        row_q, col_q, dep_q = self.decode(q % self.G)
        c_q = q // self.G
        row_s, col_s, dep_s = self.decode(s)
        row_t, _, dep_t = self.decode(s.T)
        b0 = self.rows * self.W
        select = [e == rr * self.W + row_q % self.W for rr in range(self.rows)]
        select += [e == b0 + c_q, e == b0 + self.nc + c_q, (e >= b0) & (e < b0 + c_q)]
        holds = (dep_s == dep_q) & (col_s == row_q // self.W)
        masks = [holds, s == q % self.G, col_s == col_q]
        before = np.arange(self.Q)[:, None] < q
        k = np.arange(LANES)[None, :]
        inner = (dep_q * self.nrow + row_q).T == k
        first = inner & (c_q.T == 0)
        chunk = (k.T < k) & (k.T // self.kc == k // self.kc) & (k < self.nk)
        far = s * 0 + k // self.kc != dep_s * self.ncol + col_s
        pick = [(row_s == row_t) & (dep_s == rr) for rr in range(self.rows)]
        groups = [np.concatenate(select, 1), np.concatenate(masks, 0), np.concatenate([before, inner], 1)]
        groups += [np.concatenate([chunk, first, far], 0), np.concatenate(pick, 1)]
        return [jnp.asarray(t.astype(np.float32)) for t in groups]


def entry(plan, row, place):
    lane = lax.broadcasted_iota(I32, row.shape, 1)
    return jnp.sum(jnp.where(lane == place, row, 0)) != 0


def prepare(plan, entries, b_hbm, out_hbm, tile_ref, sem, block_sems):
    def piece(c, j):
        return pltpu.make_async_copy(b_hbm.at[c], out_hbm.at[:, :, pl.ds(j * plan.bs, plan.bs)], block_sems.at[j])

    row = entries[0:1]
    count = jnp.int32(0)
    for c in range(plan.nc):
        stored = entry(plan, row, plan.rows * plan.W + c)
        for j in range(min(c + 1, plan.slots)):

            @pl.when(stored & (count == j))
            def _(c=c, j=j):
                piece(c, j).start()

        count += stored.astype(I32)

    tile_ref[...] = jnp.broadcast_to(entries[...].astype(F32)[None], tile_ref.shape)
    last = pltpu.make_async_copy(tile_ref, out_hbm.at[:, :, pl.ds(plan.slots * plan.bs, LANES)], sem.at[0])
    last.start()
    for j in range(plan.slots):

        @pl.when(count > j)
        def _(j=j):
            piece(0, j).wait()

    last.wait()


def stage(plan, entries, a_hbm, *refs):
    outs, sems = refs[:-1], refs[-1]
    dep = lax.axis_index("depth")
    row = entries[0:1]

    def each(act):
        for dd, out in enumerate(outs):
            to_dep = (dep + dd) % plan.ndep
            count = jnp.int32(0)
            for kk in range(plan.kc):
                stored = entry(plan, row, to_dep * plan.W + kk)
                at = jnp.minimum(count, plan.early - 1)

                @pl.when(stored & (count < plan.early))
                def _(dd=dd, out=out, to_dep=to_dep, kk=kk, at=at):
                    act(pltpu.make_async_copy(a_hbm.at[to_dep, kk], out.at[at], sems.at[dd, kk]))

                count += stored.astype(I32)

    each(lambda copy: copy.start())
    each(lambda copy: copy.wait())


def dot(x, y):
    return jnp.dot(x, y, preferred_element_type=F32)


def schedule(plan, p_ref, wide, masks, after, chunk, pick, table_ref, left_ref, index_ref):
    G, Q, nk = plan.G, plan.Q, plan.nk
    entries = dot(p_ref[:, 0, :], wide[...])
    holds, own, same_col = masks[0:G], masks[G : 2 * G], masks[2 * G : 3 * G]
    stored_a = jnp.zeros((G, Q), F32)
    for rr in range(plan.rows):
        stored_a += dot(pick[:, rr * G : (rr + 1) * G], entries[:, rr * Q : (rr + 1) * Q] * holds)
    b0 = plan.rows * Q
    stored_b = jnp.sum(entries[:, b0 : b0 + Q] * own, axis=0, keepdims=True)
    slot = jnp.sum(entries[:, b0 + 2 * Q : b0 + 3 * Q] * own, axis=0, keepdims=True)
    need = stored_a * stored_b * entries[:, b0 + Q : b0 + 2 * Q] * same_col
    ranks = dot(need, after[...])
    rank = ranks[:, :Q]
    left = jnp.minimum(ranks[:, Q:], 1.0)
    before, first, far = chunk[0:LANES], chunk[LANES : LANES + Q], chunk[LANES + Q :]
    stored_rank = dot(dot(stored_a, first), before)
    late = jnp.where(stored_rank >= plan.early, left, 0.0)
    late_rank = dot(late, before)
    place = jnp.where(late > 0, plan.early + late_rank, stored_rank)
    count = jnp.sum(need, axis=1, keepdims=True)
    name = slot * float(Q) + lax.broadcasted_iota(I32, (1, Q), 1).astype(F32)
    lane = lax.broadcasted_iota(I32, (G, LANES), 1)
    table = jnp.where(lane == LANES - 1, count, 0.0)
    for j in range(plan.most):
        at = jnp.sum(jnp.where(rank == float(j), need, 0.0) * name, axis=1, keepdims=True)
        table = jnp.where(lane == j, at, table)
    table_ref[...] = table.astype(I32)
    left_ref[...] = jnp.where(left > 0, place, -1.0).astype(I32)

    most = jnp.max(count)
    spread = jnp.max(need * slot) + 1.0
    if plan.whole:
        lefts = jnp.max(late * far * (late_rank + 1.0))
    else:
        lefts = jnp.float32(0)
    index = jnp.int32(len(plan.levels) - 1)
    for n in reversed(range(len(plan.levels) - 1)):
        step, few, again = plan.levels[n]
        fits = (most <= step) & (lefts <= few)
        if not again:
            fits = fits & (spread <= plan.slots)
        index = jnp.where(fits, n, index)
    index_ref[0] = index


def pack(plan, J, few, again, table, left, got_ref, a_hbm, out_ref, *refs):
    outs, sems = refs[:-1], refs[-1]
    row, col, dep = lax.axis_index("row"), lax.axis_index("col"), lax.axis_index("depth")

    def each(act):
        for o, out in enumerate(outs):
            dd, dc = plan.others[o]
            to_dep, to_col = (dep + dd) % plan.ndep, (col + dc) % plan.ncol
            member = (row * plan.ncol + to_col) * plan.ndep + to_dep
            for kk in range(plan.kc):
                place = left[member, dep * plan.nrow + col * plan.kc + kk] - plan.early

                @pl.when((place >= 0) & (place < few))
                def _():
                    at = jnp.clip(place, 0, few - 1)
                    act(pltpu.make_async_copy(a_hbm.at[to_dep, kk], out.at[at], sems.at[o, kk]))

    each(lambda copy: copy.start())

    def body(d, carry):
        for j in range(J):
            q = table[d, j]
            place = q // plan.G % plan.nc if again else q // plan.Q
            start = pl.multiple_of(place * plan.bs, plan.bs)
            out_ref[d, j] = got_ref[q % plan.G, :, pl.ds(start, plan.bs)]
        return carry

    lax.fori_loop(0, plan.G, body, 0)
    each(lambda copy: copy.wait())


def multiply(plan, J, few, table, left, got_ref, a_hbm, *refs):
    lefts, (out_hbm, a_scr, out_scr, sems, out_sems) = refs[:-5], refs[-5:]
    col, dep = lax.axis_index("col"), lax.axis_index("depth")
    member = lax.axis_index(plan.axes)
    count = table[member, LANES - 1]

    def place(j):
        q = table[member, j]
        row_s, _, dep_s = plan.decode(q % plan.G)
        return row_s, dep_s, q // plan.G % plan.nc

    def copy(src, j):
        return pltpu.make_async_copy(src, a_scr.at[j], sems.at[j])

    for j in range(J):
        row_s, dep_s, _ = place(j)
        dd = (dep - dep_s + plan.ndep) % plan.ndep
        dc = (col - row_s // plan.kc + plan.ncol) % plan.ncol
        kk = row_s % plan.kc
        for n, (xd, xc) in enumerate([(0, 0)] + plan.others):

            @pl.when((j < count) & (dd == xd) & (dc == xc))
            def _(n=n):
                if n == 0:
                    copy(a_hbm.at[dep, kk], j).start()
                elif not plan.whole:
                    copy(lefts[n - 1].at[kk], j).start()
                else:
                    at = left[member, dep_s * plan.nrow + row_s]

                    @pl.when(at < plan.early)
                    def _():
                        copy(lefts[n - 1].at[jnp.clip(at, 0, plan.early - 1)], j).start()

                    if few:

                        @pl.when(at >= plan.early)
                        def _():
                            src = lefts[len(plan.others) + n - 1]
                            copy(src.at[jnp.clip(at - plan.early, 0, few - 1)], j).start()

    out_scr[...] = jnp.zeros_like(out_scr)
    for j in range(J):

        @pl.when(j < count)
        def _():
            copy(a_hbm.at[0, 0], j).wait()
            _, _, c = place(j)
            right = got_ref[:, j].reshape(plan.bs, plan.bs)
            out_scr[c] += jnp.dot(a_scr[j], right, precision=lax.Precision.HIGHEST, preferred_element_type=F32)

    whole = pltpu.make_async_copy(out_scr, out_hbm.at[0], out_sems.at[0])
    whole.start()
    whole.wait()


def local(mesh, a_blocks, a_pattern, b_blocks, b_pattern, c_pattern):
    plan = Plan(mesh, a_blocks, b_blocks)
    G, R, bs, nc, slots = plan.G, plan.R, plan.bs, plan.nc, plan.slots
    DMA = pltpu.SemaphoreType.DMA

    def call(kernel, out_shape, in_specs, out_specs, scratch=(), **kwargs):
        name = kernel.func.__name__
        return pl.pallas_call(
            kernel,
            out_shape=out_shape,
            in_specs=in_specs,
            out_specs=out_specs,
            scratch_shapes=scratch,
            compiler_params=PARAMS,
            name=name,
            **kwargs,
        )

    def shift(value, dd, dc):
        perm = [
            (x * plan.ndep + y, (x + dc) % plan.ncol * plan.ndep + (y + dd) % plan.ndep)
            for x in range(plan.ncol)
            for y in range(plan.ndep)
        ]
        return lax.ppermute(value, ("col", "depth"), perm)

    if not plan.whole:
        a_pattern = lax.all_gather(a_pattern, "col", axis=1, tiled=True)
    entries = jnp.concatenate([x.reshape(-1) for x in (a_pattern, b_pattern, c_pattern)])
    entries = jnp.broadcast_to(jnp.pad(entries, (0, LANES - entries.size))[None], (R, LANES))

    b_pieces = b_blocks.reshape(nc, G, R, bs)
    pieces = call(
        functools.partial(prepare, plan),
        jax.ShapeDtypeStruct((G, R, slots * bs + LANES), F32),
        [VMEM, HBM],
        HBM,
        [pltpu.VMEM((G, R, LANES), F32), DMA((1,)), DMA((slots,))],
    )(entries, b_pieces)
    if plan.whole:
        staged = call(
            functools.partial(stage, plan),
            (jax.ShapeDtypeStruct((plan.early, bs, bs), F32),) * plan.ndep,
            [VMEM, HBM],
            (VMEM,) * plan.ndep,
            [DMA((plan.ndep, plan.kc))],
        )(entries, a_blocks)
    else:
        dep = lax.axis_index("depth")
        staged = [
            lax.dynamic_index_in_dim(a_blocks, (dep + dd) % plan.ndep, axis=0, keepdims=False)
            for dd in range(plan.ndep)
        ]
    early = [shift(staged[dd], dd, dc) for dd, dc in plan.others]
    got = lax.all_to_all(pieces, plan.axes, 0, 0, tiled=True)
    tables = plan.tables()
    table, left, index = call(
        functools.partial(schedule, plan),
        (
            jax.ShapeDtypeStruct((G, LANES), I32),
            jax.ShapeDtypeStruct((G, LANES), I32),
            jax.ShapeDtypeStruct((1,), I32),
        ),
        [pl.BlockSpec((G, R, LANES), lambda i: (0, 0, slots * bs // LANES))]
        + [pl.BlockSpec(t.shape, lambda i: (0, 0)) for t in tables],
        (VMEM, VMEM, SMEM),
        grid=(1,),
    )(got, *tables)
    index = index[0]
    if not plan.whole:
        index = lax.pmax(index, "col")

    def branch(J, few, again, got, table, left, a_blocks, b_pieces, *lefts):
        if again:
            got = lax.all_to_all(b_pieces.transpose(1, 2, 0, 3).reshape(G, R, nc * bs), plan.axes, 0, 0, tiled=True)
        sends = len(plan.others) if plan.whole and few else 0
        send, *chosen = call(
            functools.partial(pack, plan, J, few, again),
            (jax.ShapeDtypeStruct((G, J, R, bs), F32),) + (jax.ShapeDtypeStruct((few, bs, bs), F32),) * sends,
            [SMEM, SMEM, VMEM, HBM],
            (VMEM,) * (1 + sends),
            [DMA((len(plan.others), plan.kc))],
        )(table, left, got, a_blocks)
        lefts += tuple(shift(x, dd, dc) for x, (dd, dc) in zip(chosen, plan.others))
        blocks = lax.all_to_all(send, plan.axes, 0, 0, tiled=True)
        return call(
            functools.partial(multiply, plan, J, few),
            jax.ShapeDtypeStruct((1, nc, bs, bs), F32),
            [SMEM, SMEM, VMEM] + [HBM] * (1 + len(lefts)),
            HBM,
            [pltpu.VMEM((J, bs, bs), F32), pltpu.VMEM((nc, bs, bs), F32), DMA((J,)), DMA((1,))],
        )(table, left, blocks, a_blocks, *lefts)

    branches = [functools.partial(branch, *level) for level in plan.levels]
    return lax.switch(index, branches, got, table, left, a_blocks, b_pieces, *early)


def solution(mesh):
    in_specs = (
        P("row", ("depth", "col"), None, None),
        P("row", ("depth", "col")),
        P(("depth", "row"), "col", None, None),
        P(("depth", "row"), "col"),
        P(("row", "depth"), "col"),
    )
    out_specs = P(("row", "depth"), "col", None, None)
    return jax.shard_map(
        functools.partial(local, mesh), mesh=mesh, in_specs=in_specs, out_specs=out_specs, check_vma=False
    )
```

```python
import functools

import jax
import jax.numpy as jnp
import numpy as np
from jax import lax
from jax.experimental import pallas as pl
from jax.experimental.pallas import tpu as pltpu
from jax.sharding import PartitionSpec as P

LANES = 128
F32 = jnp.float32
BF16 = jnp.bfloat16
I32 = jnp.int32
SMEM = pl.BlockSpec(memory_space=pltpu.SMEM)
VMEM = pl.BlockSpec(memory_space=pltpu.VMEM)
HBM = pl.BlockSpec(memory_space=pltpu.HBM)
DMA = pltpu.SemaphoreType.DMA
PARAMS = pltpu.CompilerParams(vmem_limit_bytes=48 * 1024 * 1024)


class Plan:
    def __init__(self, mesh, a_blocks, b_blocks):
        self.nrow, self.ncol, self.ndep = (mesh.shape[name] for name in ("row", "col", "depth"))
        self.rows, self.kc, self.bs, _ = a_blocks.shape
        self.kb, self.nc, _, _ = b_blocks.shape
        assert self.kb == 1 and self.rows == self.ndep and self.nrow % 2 == 0
        every = self.nrow * self.ncol * self.ndep
        self.whole = self.bs // every >= 8
        self.axes = ("row", "col", "depth") if self.whole else ("row", "depth")
        self.G = every if self.whole else self.nrow * self.ndep
        self.stride = self.G // self.nrow
        self.R = self.bs // self.G
        self.Q = self.G * self.nc
        self.W = self.kc if self.whole else self.kc * self.ncol
        self.nk = self.kc * self.ncol * self.ndep
        self.most = 2 * self.nc * (self.nk // 4)
        self.J = 3 * self.nk // 16
        self.slots = self.nc - 1 if self.whole else self.nc
        self.waves = 2 if self.whole else self.kc
        assert self.G & (self.G - 1) == 0 and self.nc & (self.nc - 1) == 0
        self.g_bits, self.q_bits = self.G.bit_length() - 1, self.Q.bit_length() - 1
        self.others = [(dd, dc) for dd in range(self.ndep) for dc in range(self.ncol) if (dd, dc) != (0, 0)]

    def member(self, value):
        return (value >> 1) & (self.G - 1)

    def column(self, value):
        return (value >> (1 + self.g_bits)) & (self.nc - 1)

    def slot(self, value):
        return value >> (1 + self.q_bits)

    def decode(self, s):
        if self.whole:
            return s // (self.ncol * self.ndep), s // self.ndep % self.ncol, s % self.ndep
        return s // self.ndep, s * 0, s % self.ndep

    def tables(self):
        q = np.arange(self.Q)[None, :]
        s = np.arange(self.G)[:, None]
        e = np.arange(LANES)[:, None]
        row_q, col_q, dep_q = self.decode(q % self.G)
        c_q = q // self.G
        row_s, col_s, dep_s = self.decode(s)
        row_t, col_t, dep_t = self.decode(s.T)
        b0 = self.rows * self.W
        select = [e == rr * self.W + row_q % self.W for rr in range(self.rows)]
        select += [e == b0 + c_q, e == b0 + self.nc + c_q, (e >= b0) & (e < b0 + c_q)]
        holds = (dep_s == dep_q) & (col_s == row_q // self.W)
        masks = [holds, s == q % self.G, col_s == col_q]
        before = np.arange(self.Q)[:, None] < q
        k = np.arange(LANES)[None, :]
        inner = (dep_q * self.nrow + row_q).T == k
        first = inner & (c_q.T == 0) & (col_q.T == 0)
        chunk = (k.T < k) & (k.T // self.kc == k // self.kc) & (k < self.nk)
        pick = [(row_s == row_t) & (dep_s == rr) for rr in range(self.rows)]
        pick += [(row_s // 2 == row_t // 2) & (col_s == col_t) & (dep_s == dep_t)]
        groups = [np.concatenate(select, 1), np.concatenate(masks, 0), before]
        far = (k // self.kc != dep_s * self.ncol + col_s) | (not self.whole)
        groups += [np.concatenate([inner, first], 1), np.concatenate([chunk, far], 0), np.concatenate(pick, 1)]
        return [jnp.asarray(t.astype(np.float32), BF16) for t in groups]


def dot(x, y):
    return jnp.dot(x.astype(BF16), y.astype(BF16), preferred_element_type=F32)


def dot_high(x, y):
    x_high, y_high = x.astype(BF16), y.astype(BF16)
    x_low, y_low = (x - x_high.astype(F32)).astype(BF16), (y - y_high.astype(F32)).astype(BF16)
    return dot(x_high, y_low) + dot(x_low, y_high) + dot(x_high, y_high)


def entry_row(plan, entries):
    row = entries[0:1]
    for r in range(1, plan.rows):
        row += pltpu.roll(entries[r : r + 1], r * plan.W, 1)
    return row


def entry(row, place):
    lane = lax.broadcasted_iota(I32, row.shape, 1)
    return jnp.sum(jnp.where(lane == place, row, 0)) != 0


def prepare(plan, entries, b_hbm, out_ref, sems):
    def piece(c, j):
        return pltpu.make_async_copy(b_hbm.at[c], out_ref.at[:, :, pl.ds(j * plan.bs, plan.bs)], sems.at[j])

    row = entry_row(plan, entries)
    count = jnp.int32(0)
    for c in range(plan.nc):
        stored = entry(row, plan.rows * plan.W + c)
        for j in range(min(c + 1, plan.slots)):

            @pl.when(stored & (count == j))
            def _(c=c, j=j):
                piece(c, j).start()

        count += stored.astype(I32)

    tile = jnp.broadcast_to(row.astype(F32)[None], (plan.G, plan.R, LANES))
    out_ref[:, :, plan.slots * plan.bs :] = tile
    for j in range(plan.slots):

        @pl.when(count > j)
        def _(j=j):
            piece(0, j).wait()


def stage(plan, wave, entries, a_hbm, *refs):
    outs, sems = refs[:-1], refs[-1]
    col, dep = lax.axis_index("col"), lax.axis_index("depth")
    row = entry_row(plan, entries)
    start = 0 if plan.whole else col * plan.kc
    stored = [[entry(row, r * plan.W + start + kk) for kk in range(plan.kc)] for r in range(plan.rows)]

    def each(act):
        for r in range(plan.rows):
            count = jnp.int32(0)
            for kk in range(plan.kc):
                for dd, out in enumerate(outs):

                    @pl.when(stored[r][kk] & (count == wave) & ((dep + dd) % plan.ndep == r))
                    def _(r=r, kk=kk, out=out):
                        act(pltpu.make_async_copy(a_hbm.at[r, kk], out, sems.at[r]))

                count += stored[r][kk].astype(I32)

    each(lambda copy: copy.start())
    each(lambda copy: copy.wait())


def stage_needed(plan, wave, left, a_hbm, *refs):
    outs, sems = refs[:-1], refs[-1]
    row, col, dep = lax.axis_index("row"), lax.axis_index("col"), lax.axis_index("depth")

    def each(act):
        for o, out in enumerate(outs):
            dd, dc = plan.others[o]
            to_dep, to_col = (dep + dd) % plan.ndep, (col + dc) % plan.ncol
            member = (row * plan.ncol + to_col) * plan.ndep + to_dep
            for kk in range(plan.kc):

                @pl.when(left[member, dep * plan.nrow + col * plan.kc + kk] == wave)
                def _(o=o, kk=kk, out=out, to_dep=to_dep):
                    act(pltpu.make_async_copy(a_hbm.at[to_dep, kk], out, sems.at[o]))

    each(lambda copy: copy.start())
    each(lambda copy: copy.wait())


def needs(plan, tile, wide, masks, before, inner, chunk, pick):
    G, Q, rows = plan.G, plan.Q, plan.rows
    entries = dot(tile, wide[...])
    holds, own, same_col = masks[0:G], masks[G : 2 * G], masks[2 * G : 3 * G]
    stored_a = jnp.zeros((G, Q), F32)
    for rr in range(rows):
        stored_a += dot(pick[:, rr * G : (rr + 1) * G], entries[:, rr * Q : (rr + 1) * Q] * holds)
    b0 = rows * Q
    stored_b = jnp.sum(entries[:, b0 : b0 + Q] * own, axis=0, keepdims=True)
    slot = jnp.sum(entries[:, b0 + 2 * Q : b0 + 3 * Q] * own, axis=0, keepdims=True)
    need = stored_a * stored_b * entries[:, b0 + Q : b0 + 2 * Q] * same_col
    both = jnp.minimum(dot(pick[:, rows * G :], need), 1.0)
    rank = dot(both, before[...])
    before_k, far = chunk[0:LANES], chunk[LANES:]
    left = jnp.minimum(dot(need, inner[:, :LANES]), 1.0)
    place = dot(dot(stored_a, inner[:, LANES:]), before_k)
    if plan.whole:
        late = jnp.where(place > 0, left, 0.0)
        place = jnp.where(place > 0, jnp.where(late > 0, 1.0 + dot(late, before_k), -1.0), 0.0)
    name = slot * float(Q) + lax.broadcasted_iota(I32, (1, Q), 1).astype(F32)
    most = jnp.max(jnp.sum(both, axis=1, keepdims=True))
    lost = jnp.max(need * jnp.where(slot >= plan.slots, 1.0, 0.0))
    waves = jnp.max(left * far * (place + 1.0))
    return need, both, rank, name, place, most, lost, waves


def list_blocks(plan, count, need, both, rank, name):
    lane = lax.broadcasted_iota(I32, (plan.G, LANES), 1)
    value = both * name * 2.0 + need
    table = jnp.zeros((plan.G, LANES), F32)
    for j in range(count):
        at = jnp.sum(jnp.where(rank == float(j), value, 0.0) * both, axis=1, keepdims=True)
        table = jnp.where(lane == j, at, table)
    return table.astype(I32)


def fill(plan, again, base, table, got_ref, out_ref):
    def body(d, carry):
        core = (d // plan.stride) & 1
        for p in range(plan.J):
            value = table[d, base + 2 * p + core]
            slot = plan.column(value) if again else plan.slot(value)
            start = pl.multiple_of(slot * plan.bs, plan.bs)
            out_ref[d, p] = got_ref[plan.member(value), :, pl.ds(start, plan.bs)]
        return carry

    lax.fori_loop(0, plan.G, body, 0, unroll=4)


def schedule(plan, got_ref, *refs):
    tables, (out_ref, table_ref, left_ref, state_ref, scratch, sem) = refs[:6], refs[-6:]
    tile = got_ref[:, 0, plan.slots * plan.bs :]
    need, both, rank, name, place, most, lost, waves = needs(plan, tile, *tables)
    table_ref[...] = list_blocks(plan, 2 * plan.J, need, both, rank, name)
    copy = pltpu.make_async_copy(table_ref, scratch, sem.at[0])
    copy.start()
    left_ref[...] = place.astype(I32)
    more = most > 2 * plan.J
    wave = waves > plan.waves
    again = (lost > 0) | (waves > plan.waves + 1) | (wave & more)
    state_ref[0] = jnp.where(again, 3, jnp.where(wave, 2, jnp.where(more, 1, 0)))
    copy.wait()
    fill(plan, False, 0, scratch, got_ref, out_ref)


def relist(plan, tile_ref, *refs):
    tables, (table_ref, rounds_ref) = refs[:-2], refs[-2:]
    need, both, rank, name, _, most, _, _ = needs(plan, tile_ref[:, 0, :], *tables)
    table_ref[...] = list_blocks(plan, plan.most, need, both, rank, name)
    rounds_ref[0] = (most.astype(I32) + 2 * plan.J - 1) // (2 * plan.J)


def pack(plan, again, turn, table, got_ref, out_ref):
    fill(plan, again, turn[0] * (2 * plan.J), table, got_ref, out_ref)


def multiply(plan, again, waves, first, turn, table, left, mine, theirs, a_hbm, *refs):
    lefts, refs = refs[: waves * len(plan.others)], refs[waves * len(plan.others) :]
    start_refs, (out_hbm, a_scr, right, total, sems, out_sem) = refs[:-6], refs[-6:]
    col, dep = lax.axis_index("col"), lax.axis_index("depth")
    member = lax.axis_index(plan.axes)
    core = (member // plan.stride) & 1
    base = 0 if first else turn[0] * (2 * plan.J)
    listed = [table[member, base + j] for j in range(2 * plan.J)]

    def copy(src, j):
        return pltpu.make_async_copy(src, a_scr.at[j], sems.at[j])

    ready = []
    for j, value in enumerate(listed):
        row_s, _, dep_s = plan.decode(plan.member(value))
        dd = (dep - dep_s + plan.ndep) % plan.ndep
        dc = (col - row_s // plan.kc + plan.ncol) % plan.ncol
        kk = row_s % plan.kc
        wave = jnp.int32(0) if again else left[member, dep_s * plan.nrow + row_s]
        ready.append((value & 1 == 1) & (((dd == 0) & (dc == 0)) | (wave < waves)))
        for n, (xd, xc) in enumerate([(0, 0)] + plan.others):
            here = ready[j] & (dd == xd) & (dc == xc)
            for w in range(waves if n else 1):

                @pl.when(here & (wave == w) if n else here)
                def _(n=n, j=j, kk=kk, w=w):
                    src = lefts[w * len(plan.others) + n - 1]
                    copy(a_hbm.at[dep, kk] if n == 0 else src.at[kk] if again else src, j).start()

    if first:
        total[...] = jnp.zeros_like(total)
    else:
        begin = pltpu.make_async_copy(start_refs[0].at[0], total, out_sem.at[0])
        begin.start()
        begin.wait()
    for j, value in enumerate(listed):

        @pl.when(ready[j])
        def _(j=j, value=value):
            @pl.when(core == j % 2)
            def _():
                right[...] = mine[:, j // 2].reshape(plan.bs, plan.bs)

            @pl.when(core != j % 2)
            def _():
                right[...] = theirs[:, j // 2].reshape(plan.bs, plan.bs)

            copy(a_hbm.at[0, 0], j).wait()
            c = plan.column(value)
            total[c] += dot_high(a_scr[j], right[...])

    end = pltpu.make_async_copy(total, out_hbm.at[0], out_sem.at[0])
    end.start()
    end.wait()


def call(kernel, out_shape, in_specs, out_specs, scratch=(), **kwargs):
    return pl.pallas_call(
        kernel,
        out_shape=out_shape,
        in_specs=in_specs,
        out_specs=out_specs,
        scratch_shapes=scratch,
        compiler_params=PARAMS,
        name=kernel.func.__name__,
        **kwargs,
    )


def local(mesh, a_blocks, a_pattern, b_blocks, b_pattern, c_pattern):
    plan = Plan(mesh, a_blocks, b_blocks)
    G, R, J, bs, nc = plan.G, plan.R, plan.J, plan.bs, plan.nc
    listing = jax.ShapeDtypeStruct((G, LANES), I32)
    flag = jax.ShapeDtypeStruct((1,), I32)
    sending = jax.ShapeDtypeStruct((G, J, R, bs), F32)

    def exchange(pieces):
        return lax.all_to_all(pieces, plan.axes, 0, 0, tiled=True)

    def shift(staged):
        def perm(dd, dc):
            for x in range(plan.ncol):
                for y in range(plan.ndep):
                    yield x * plan.ndep + y, (x + dc) % plan.ncol * plan.ndep + (y + dd) % plan.ndep

        return [lax.ppermute(x, ("col", "depth"), list(perm(*by))) for x, by in zip(staged, plan.others)]

    def wave_of(kernel, given, a_blocks, distinct):
        out = call(
            kernel,
            (jax.ShapeDtypeStruct((bs, bs), F32),) * distinct,
            [SMEM if kernel.func is stage_needed else VMEM, HBM],
            (VMEM,) * distinct,
            [DMA((distinct,))],
        )(given, a_blocks)
        return shift(out if kernel.func is stage_needed else [out[dd] for dd, _ in plan.others])

    def swap(mine):
        return lax.ppermute(mine, "row", [(i, i ^ 1) for i in range(plan.nrow)])

    def product(again, turn, table, left, mine, theirs, a_blocks, lefts, start=None):
        starts = [] if start is None else [start]
        return call(
            functools.partial(multiply, plan, again, len(lefts) // len(plan.others), start is None),
            jax.ShapeDtypeStruct((1, nc, bs, bs), F32),
            [SMEM, SMEM, SMEM, VMEM, VMEM] + [HBM] * (1 + len(lefts) + len(starts)),
            HBM,
            [
                pltpu.VMEM((2 * J, bs, bs), F32),
                pltpu.VMEM((bs, bs), F32),
                pltpu.VMEM((nc, bs, bs), F32),
                DMA((2 * J,)),
                DMA((1,)),
            ],
        )(turn, table, left, mine, theirs, a_blocks, *lefts, *starts)

    if not plan.whole:
        a_pattern = lax.all_gather(a_pattern, "col", axis=1, tiled=True)
    b0 = plan.rows * plan.W
    entries = jnp.pad(b_pattern, ((0, plan.rows - 1), (b0, LANES - b0 - nc)))
    entries += jnp.pad(c_pattern, ((0, plan.rows - 1), (b0 + nc, LANES - b0 - 2 * nc)))
    entries += jnp.pad(a_pattern, ((0, 0), (0, LANES - plan.W)))

    b_pieces = b_blocks.reshape(nc, G, R, bs)
    width = plan.slots * bs + LANES
    pieces = call(
        functools.partial(prepare, plan),
        jax.ShapeDtypeStruct((G, R, width), F32),
        [VMEM, HBM],
        VMEM,
        [DMA((plan.slots,))],
    )(entries, b_pieces)
    got = exchange(pieces)
    early = 1 if plan.whole else plan.waves
    lefts = []
    for wave in range(early):
        lefts += wave_of(functools.partial(stage, plan, wave), entries, a_blocks, plan.ndep)

    tables = plan.tables()
    beside = lefts
    send, table, left, state = call(
        functools.partial(schedule, plan),
        (sending, listing, listing, flag),
        [VMEM] * (1 + len(tables)) + [HBM] * len(beside),
        (VMEM, VMEM, VMEM, SMEM),
        [pltpu.SMEM((G, LANES), I32), DMA((1,))],
    )(got, *tables, *beside)
    mine = exchange(send)
    if plan.whole:
        late = wave_of(functools.partial(stage_needed, plan, 1), left, a_blocks, len(plan.others))
        mine, late = lax.optimization_barrier((mine, late))
        lefts = lefts + late
    theirs = swap(mine)
    c_blocks = product(False, state, table, left, mine, theirs, a_blocks, lefts)

    def rounds(again, got, pieces, left, a_blocks, lefts, first, c_blocks):
        table, total = call(
            functools.partial(relist, plan),
            (listing, flag),
            [pl.BlockSpec((G, R, LANES), lambda i: (0, 0, plan.slots * bs // LANES))]
            + [pl.BlockSpec(t.shape, lambda i: (0, 0)) for t in tables],
            (VMEM, SMEM),
            grid=(1,),
        )(got, *tables)
        total = total[0] if plan.whole else lax.pmax(total[0], "col")

        def body(turn, c_blocks):
            turn = jnp.reshape(turn, (1,))
            send = call(functools.partial(pack, plan, again), sending, [SMEM, SMEM, VMEM], VMEM)(turn, table, pieces)
            mine = exchange(send)
            return product(again, turn, table, left, mine, swap(mine), a_blocks, lefts, c_blocks)

        return lax.fori_loop(first, total, body, c_blocks)

    def done(c_blocks, *_):
        return c_blocks

    def more_rounds(c_blocks, mine, theirs, got, table, left, a_blocks, b_pieces, *lefts):
        return rounds(False, got, got, left, a_blocks, lefts, 1, c_blocks)

    def more_waves(c_blocks, mine, theirs, got, table, left, a_blocks, b_pieces, *lefts):
        if plan.whole:
            lefts += tuple(wave_of(functools.partial(stage_needed, plan, 2), left, a_blocks, len(plan.others)))
        return product(False, jnp.zeros((1,), I32), table, left, mine, theirs, a_blocks, lefts)

    def anew(c_blocks, mine, theirs, got, table, left, a_blocks, b_pieces, *lefts):
        pieces = exchange(b_pieces.transpose(1, 2, 0, 3).reshape(G, R, nc * bs))
        dep = lax.axis_index("depth")
        raw = [lax.dynamic_index_in_dim(a_blocks, (dep + dd) % plan.ndep, keepdims=False) for dd, _ in plan.others]
        return rounds(True, got, pieces, left, a_blocks, shift(raw), 0, jnp.zeros_like(c_blocks))

    index = state[0] if plan.whole else lax.pmax(state[0], "col")
    branches = [done, more_rounds, more_waves, anew]
    return lax.switch(index, branches, c_blocks, mine, theirs, got, table, left, a_blocks, b_pieces, *lefts)


def solution(mesh):
    in_specs = (
        P("row", ("depth", "col"), None, None),
        P("row", ("depth", "col")),
        P(("depth", "row"), "col", None, None),
        P(("depth", "row"), "col"),
        P(("row", "depth"), "col"),
    )
    out_specs = P(("row", "depth"), "col", None, None)
    return jax.shard_map(
        functools.partial(local, mesh), mesh=mesh, in_specs=in_specs, out_specs=out_specs, check_vma=False
    )
```

```python
import functools

import jax
import jax.numpy as jnp
import numpy as np
from jax import lax
from jax.experimental import pallas as pl
from jax.experimental.pallas import tpu as pltpu
from jax.sharding import PartitionSpec as P

LANES = 128
F32 = jnp.float32
BF16 = jnp.bfloat16
I32 = jnp.int32
SMEM = pl.BlockSpec(memory_space=pltpu.SMEM)
VMEM = pl.BlockSpec(memory_space=pltpu.VMEM)
HBM = pl.BlockSpec(memory_space=pltpu.HBM)
DMA = pltpu.SemaphoreType.DMA
PARAMS = pltpu.CompilerParams(vmem_limit_bytes=48 * 1024 * 1024)


class Plan:
    def __init__(self, mesh, a_blocks, b_blocks):
        self.nrow, self.ncol, self.ndep = (mesh.shape[name] for name in ("row", "col", "depth"))
        self.rows, self.kc, self.bs, _ = a_blocks.shape
        self.kb, self.nc, _, _ = b_blocks.shape
        assert self.kb == 1 and self.rows == self.ndep and self.nrow % 2 == 0
        every = self.nrow * self.ncol * self.ndep
        self.whole = self.bs // every >= 8
        self.axes = ("row", "col", "depth") if self.whole else ("row", "depth")
        self.G = every if self.whole else self.nrow * self.ndep
        self.stride = self.G // self.nrow
        self.R = self.bs // self.G
        self.Q = self.G * self.nc
        self.W = self.kc if self.whole else self.kc * self.ncol
        self.nk = self.kc * self.ncol * self.ndep
        self.J = 3 * self.nk // 16
        self.slots = self.nc - 1 if self.whole else self.nc
        self.waves = 2 if self.whole else self.kc
        assert self.G & (self.G - 1) == 0 and self.nc & (self.nc - 1) == 0
        self.g_bits, self.q_bits = self.G.bit_length() - 1, self.Q.bit_length() - 1
        self.others = [(dd, dc) for dd in range(self.ndep) for dc in range(self.ncol) if (dd, dc) != (0, 0)]

    def member(self, value):
        return (value >> 2) & (self.G - 1)

    def column(self, value):
        return (value >> (2 + self.g_bits)) & (self.nc - 1)

    def slot(self, value):
        return value >> (2 + self.q_bits)

    def listed(self, rows, p, member):
        per = LANES // self.G
        return rows[p // per, p % per * self.G + member]

    def decode(self, s):
        if self.whole:
            return s // (self.ncol * self.ndep), s // self.ndep % self.ncol, s % self.ndep
        return s // self.ndep, s * 0, s % self.ndep

    def tables(self):
        q = np.arange(self.Q)[None, :]
        s = np.arange(self.G)[:, None]
        e = np.arange(LANES)[:, None]
        row_q, col_q, dep_q = self.decode(q % self.G)
        c_q = q // self.G
        row_s, col_s, dep_s = self.decode(s)
        row_t, col_t, dep_t = self.decode(s.T)
        b0 = self.rows * self.W
        select = [e == rr * self.W + row_q % self.W for rr in range(self.rows)]
        select += [e == b0 + c_q, e == b0 + self.nc + c_q, (e >= b0) & (e < b0 + c_q)]
        holds = (dep_s == dep_q) & (col_s == row_q // self.W)
        masks = [holds, s == q % self.G, col_s == col_q]
        before = np.arange(self.Q)[:, None] < q
        k = np.arange(LANES)[None, :]
        inner = (dep_q * self.nrow + row_q).T == k
        first = inner & (c_q.T == 0) & (col_q.T == 0)
        chunk = (k.T < k) & (k.T // self.kc == k // self.kc) & (k < self.nk)
        pick = [(row_s == row_t) & (dep_s == rr) for rr in range(self.rows)]
        pick += [(row_s ^ 1 == row_t) & (col_s == col_t) & (dep_s == dep_t)]
        groups = [np.concatenate(select, 1), np.concatenate(masks, 0), before, np.concatenate(pick, 1)]
        far = (k // self.kc != dep_s * self.ncol + col_s) | (not self.whole)
        groups += [np.concatenate([inner, first], 1), np.concatenate([chunk, far], 0)]
        return [jnp.asarray(t.astype(np.float32), BF16) for t in groups]


def dot(x, y):
    return jnp.dot(x.astype(BF16), y.astype(BF16), preferred_element_type=F32)


def dot_high(x, y):
    x_high, y_high = x.astype(BF16), y.astype(BF16)
    x_low, y_low = (x - x_high.astype(F32)).astype(BF16), (y - y_high.astype(F32)).astype(BF16)
    return dot(x_high, y_low) + dot(x_low, y_high) + dot(x_high, y_high)


def entry_row(plan, entries):
    row = entries[0:1]
    for r in range(1, plan.rows):
        row += pltpu.roll(entries[r : r + 1], r * plan.W, 1)
    return row


def entry(row, place):
    lane = lax.broadcasted_iota(I32, row.shape, 1)
    return jnp.sum(jnp.where(lane == place, row, 0)) != 0


def prepare(plan, entries, b_hbm, out_ref, sems):
    def piece(c, j):
        return pltpu.make_async_copy(b_hbm.at[c], out_ref.at[:, :, pl.ds(j * plan.bs, plan.bs)], sems.at[j])

    row = entry_row(plan, entries)
    count = jnp.int32(0)
    for c in range(plan.nc):
        stored = entry(row, plan.rows * plan.W + c)
        for j in range(min(c + 1, plan.slots)):

            @pl.when(stored & (count == j))
            def _(c=c, j=j):
                piece(c, j).start()

        count += stored.astype(I32)

    tile = jnp.broadcast_to(row.astype(F32)[None], (plan.G, plan.R, LANES))
    out_ref[:, :, plan.slots * plan.bs :] = tile
    for j in range(plan.slots):

        @pl.when(count > j)
        def _(j=j):
            piece(0, j).wait()


def stage(plan, wave, entries, a_hbm, *refs):
    outs, sems = refs[:-1], refs[-1]
    col, dep = lax.axis_index("col"), lax.axis_index("depth")
    row = entry_row(plan, entries)
    start = 0 if plan.whole else col * plan.kc
    stored = [[entry(row, r * plan.W + start + kk) for kk in range(plan.kc)] for r in range(plan.rows)]

    def each(act):
        for r in range(plan.rows):
            count = jnp.int32(0)
            for kk in range(plan.kc):
                for dd, out in enumerate(outs):

                    @pl.when(stored[r][kk] & (count == wave) & ((dep + dd) % plan.ndep == r))
                    def _(r=r, kk=kk, out=out):
                        act(pltpu.make_async_copy(a_hbm.at[r, kk], out, sems.at[r]))

                count += stored[r][kk].astype(I32)

    each(lambda copy: copy.start())
    each(lambda copy: copy.wait())


def needs(plan, tile, wide, masks, before, pick):
    G, Q, rows = plan.G, plan.Q, plan.rows
    entries = dot(tile, wide[...])
    holds, own, same_col = masks[0:G], masks[G : 2 * G], masks[2 * G : 3 * G]
    stored_a = jnp.zeros((G, Q), F32)
    for rr in range(rows):
        stored_a += dot(pick[:, rr * G : (rr + 1) * G], entries[:, rr * Q : (rr + 1) * Q] * holds)
    b0 = rows * Q
    stored_b = jnp.sum(entries[:, b0 : b0 + Q] * own, axis=0, keepdims=True)
    slot = jnp.sum(entries[:, b0 + 2 * Q : b0 + 3 * Q] * own, axis=0, keepdims=True)
    need = stored_a * stored_b * entries[:, b0 + Q : b0 + 2 * Q] * same_col
    partner = dot(pick[:, rows * G :], need)
    both = jnp.maximum(need, partner)
    return need, partner, both, dot(both, before[...]), slot, stored_a


def list_blocks(plan, base, need, partner, both, rank, slot, out):
    G, Q, per = plan.G, plan.Q, LANES // plan.G
    q = lax.broadcasted_iota(I32, (1, Q), 1).astype(F32)
    value = 4.0 * both * (slot * float(Q) + q) + 2.0 * partner + need
    member = lax.broadcasted_iota(I32, (G, LANES), 0)
    lane = lax.broadcasted_iota(I32, (G, LANES), 1)
    turn = rank - ((member[:, :1] >> (plan.stride.bit_length() - 1)) & 1).astype(F32) - base
    for n in range(out.shape[0]):
        row = jnp.zeros((G, LANES), F32)
        for p in range(n * per, min((n + 1) * per, plan.J)):
            at = jnp.sum(jnp.where(turn == 2.0 * p, value, 0.0), axis=1, keepdims=True)
            row = jnp.where(lane == p % per * G + member, at, row)
        out[n : n + 1] = jnp.sum(row, axis=0, keepdims=True).astype(I32)


def fill(plan, again, rows, got_ref, out_ref):
    for p in range(plan.J):

        def body(d, carry, p=p):
            value = plan.listed(rows, p, d)
            slot = plan.column(value) if again else plan.slot(value)
            start = pl.multiple_of(slot * plan.bs, plan.bs)
            out_ref[d, p] = got_ref[plan.member(value), :, pl.ds(start, plan.bs)]
            return carry

        lax.fori_loop(0, plan.G, body, 0, unroll=8)


def schedule(plan, again, turn, tile_ref, got_ref, *refs):
    tables, (out_ref, rows_ref, scratch, sem) = refs[:4], refs[-4:]
    base = (turn[0] * (2 * plan.J)).astype(F32)
    need, partner, both, rank, slot, _ = needs(plan, tile_ref[:, 0, tile_ref.shape[2] - LANES :], *tables)
    list_blocks(plan, base, need, partner, both, rank, slot, rows_ref)
    copy = pltpu.make_async_copy(rows_ref, scratch, sem.at[0])
    copy.start()
    copy.wait()
    fill(plan, again, scratch, got_ref, out_ref)


def settle(plan, wave, got_ref, *refs):
    tables, (inner, chunk, a_hbm), refs = refs[:4], refs[4:7], refs[7:]
    outs, (waves_ref, state_ref, zero_hbm, place_ref, place_smem, zero, sems, zero_sems) = refs[:-8], refs[-8:]
    zero[...] = jnp.zeros_like(zero)
    clear = [pltpu.make_async_copy(zero, zero_hbm.at[0, c], zero_sems.at[c]) for c in range(plan.nc)]
    for copy in clear:
        copy.start()
    need, _, both, _, slot, stored_a = needs(plan, got_ref[:, 0, got_ref.shape[2] - LANES :], *tables)
    before, far = chunk[0:LANES], chunk[LANES:]
    left = jnp.minimum(dot(need, inner[:, :LANES]), 1.0)
    place = dot(dot(stored_a, inner[:, LANES:]), before)
    if plan.whole:
        late = jnp.where(place > 0, left, 0.0)
        place = jnp.where(place > 0, jnp.where(late > 0, 1.0 + dot(late, before), -1.0), 0.0)
    place_ref[...] = place.astype(I32)
    fetch = pltpu.make_async_copy(place_ref, place_smem, sems.at[len(outs)])
    fetch.start()
    member = lax.axis_index(plan.axes)
    mine = lax.broadcasted_iota(I32, place.shape, 0) == member
    waves_ref[...] = jnp.sum(jnp.where(mine, place, 0.0), axis=0, keepdims=True).astype(I32)
    rounds = (jnp.max(jnp.sum(both, axis=1, keepdims=True)).astype(I32) + 2 * plan.J - 1) // (2 * plan.J)
    lost = jnp.max(need * jnp.where(slot >= plan.slots, 1.0, 0.0)) > 0
    waves = jnp.max(left * far * (place + 1.0))
    easy = jnp.where(lost, 3, jnp.where(rounds > 1, 1, 0))
    hard = jnp.where((waves > plan.waves + 1) | (easy > 0), 4, 2)
    state_ref[0] = jnp.where(waves > plan.waves, hard, easy)
    state_ref[1] = rounds

    row, col, dep = lax.axis_index("row"), lax.axis_index("col"), lax.axis_index("depth")

    def each(act):
        for o, out in enumerate(outs):
            dd, dc = plan.others[o]
            to_dep, to_col = (dep + dd) % plan.ndep, (col + dc) % plan.ncol
            to = (row * plan.ncol + to_col) * plan.ndep + to_dep
            for kk in range(plan.kc):

                @pl.when(place_smem[to, dep * plan.nrow + col * plan.kc + kk] == wave)
                def _(o=o, kk=kk, out=out, to_dep=to_dep):
                    act(pltpu.make_async_copy(a_hbm.at[to_dep, kk], out, sems.at[o]))

    fetch.wait()
    each(lambda copy: copy.start())
    each(lambda copy: copy.wait())
    for copy in clear:
        copy.wait()


def multiply(plan, raw, waves, first, rows, left, mine, theirs, a_hbm, *refs):
    lefts, refs = refs[: waves * len(plan.others)], refs[waves * len(plan.others) :]
    _, out_hbm, a_scr, right, total, sems, out_sems = refs
    col, dep = lax.axis_index("col"), lax.axis_index("depth")
    member = lax.axis_index(plan.axes)
    listed = [plan.listed(rows, p, member) for p in range(plan.J)]
    listed += [plan.listed(rows, p, member ^ plan.stride) >> 1 << 1 for p in range(plan.J)]
    asked = [value & 1 for value in listed[: plan.J]] + [(value >> 1) & 1 for value in listed[plan.J :]]

    def copy(src, j):
        return pltpu.make_async_copy(src, a_scr.at[j], sems.at[j])

    ready = []
    for j, value in enumerate(listed):
        row_s, _, dep_s = plan.decode(plan.member(value))
        dd = (dep - dep_s + plan.ndep) % plan.ndep
        dc = (col - row_s // plan.kc + plan.ncol) % plan.ncol
        kk = row_s % plan.kc
        near = (dd == 0) & (dc == 0)
        wave = jnp.int32(0) if raw else left[0, dep_s * plan.nrow + row_s]
        ready.append((asked[j] == 1) & (near | (wave < waves)))

        @pl.when(ready[j])
        def _(j=j, kk=kk, dd=dd, dc=dc, near=near, wave=wave):
            @pl.when(near)
            def _():
                copy(a_hbm.at[dep, kk], j).start()

            for n, (xd, xc) in enumerate(plan.others):
                for w in range(waves):

                    @pl.when((dd == xd) & (dc == xc) & (wave == w))
                    def _(n=n, w=w):
                        src = lefts[w * len(plan.others) + n]
                        copy(src.at[kk] if raw else src, j).start()

    def block(c):
        return pltpu.make_async_copy(total.at[c], out_hbm.at[0, c], out_sems.at[c])

    column = [plan.column(value) for value in listed]
    touched = [functools.reduce(jnp.logical_or, [r & (x == c) for r, x in zip(ready, column)]) for c in range(plan.nc)]
    for c in range(plan.nc):

        @pl.when(touched[c])
        def _(c=c):
            if first:
                total[c] = jnp.zeros((plan.bs, plan.bs), F32)
            else:
                begin = pltpu.make_async_copy(out_hbm.at[0, c], total.at[c], out_sems.at[c])
                begin.start()
                begin.wait()

    for j in range(2 * plan.J):

        @pl.when(ready[j])
        def _(j=j):
            source = mine if j < plan.J else theirs
            right[...] = source[:, j % plan.J].reshape(plan.bs, plan.bs)
            copy(a_hbm.at[0, 0], j).wait()
            total[column[j]] += dot_high(a_scr[j], right[...])

    for act in (lambda copy: copy.start(), lambda copy: copy.wait()):
        for c in range(plan.nc):
            pl.when(touched[c])(lambda c=c, act=act: act(block(c)))


def call(kernel, out_shape, in_specs, out_specs, scratch=(), **kwargs):
    return pl.pallas_call(
        kernel,
        out_shape=out_shape,
        in_specs=in_specs,
        out_specs=out_specs,
        scratch_shapes=scratch,
        compiler_params=PARAMS,
        name=kernel.func.__name__,
        **kwargs,
    )


def local(mesh, a_blocks, a_pattern, b_blocks, b_pattern, c_pattern):
    plan = Plan(mesh, a_blocks, b_blocks)
    G, R, J, bs, nc = plan.G, plan.R, plan.J, plan.bs, plan.nc
    result = jax.ShapeDtypeStruct((1, nc, bs, bs), F32)
    block = jax.ShapeDtypeStruct((bs, bs), F32)
    listing = (-(-J * G // LANES), LANES)

    def exchange(pieces):
        return lax.all_to_all(pieces, plan.axes, 0, 0, tiled=True)

    def shift(staged):
        def perm(dd, dc):
            for x in range(plan.ncol):
                for y in range(plan.ndep):
                    yield x * plan.ndep + y, (x + dc) % plan.ncol * plan.ndep + (y + dd) % plan.ndep

        return [lax.ppermute(x, ("col", "depth"), list(perm(*by))) for x, by in zip(staged, plan.others)]

    def swap(mine):
        return lax.ppermute(mine, "row", [(i, i ^ 1) for i in range(plan.nrow)])

    def listed(again, turn, got, pieces):
        send, rows = call(
            functools.partial(schedule, plan, again),
            (jax.ShapeDtypeStruct((G, J, R, bs), F32), jax.ShapeDtypeStruct(listing, I32)),
            [SMEM] + [VMEM] * 6,
            (VMEM, VMEM),
            [pltpu.SMEM(listing, I32), DMA((1,))],
        )(jnp.reshape(turn, (1,)), got, pieces, *tables[:4])
        return rows, lax.all_to_all(send, plan.axes, 0, 0, tiled=True)

    def settled(wave, got, a_blocks):
        count = len(plan.others) if plan.whole else 0
        *late, waves, state, zero = call(
            functools.partial(settle, plan, wave),
            (block,) * count
            + (jax.ShapeDtypeStruct((1, LANES), I32), jax.ShapeDtypeStruct((2,), I32), result),
            [VMEM] * 7 + [HBM],
            (VMEM,) * count + (VMEM, SMEM, HBM),
            [
                pltpu.VMEM((G, LANES), I32),
                pltpu.SMEM((G, LANES), I32),
                pltpu.VMEM((bs, bs), F32),
                DMA((count + 1,)),
                DMA((nc,)),
            ],
        )(got, *tables, a_blocks)
        return shift(late), waves, state, zero

    def product(raw, first, rows, waves, mine, theirs, a_blocks, lefts, start):
        return call(
            functools.partial(multiply, plan, raw, len(lefts) // len(plan.others), first),
            result,
            [SMEM, SMEM, VMEM, VMEM] + [HBM] * (2 + len(lefts)),
            HBM,
            [
                pltpu.VMEM((2 * J, bs, bs), F32),
                pltpu.VMEM((bs, bs), F32),
                pltpu.VMEM((nc, bs, bs), F32),
                DMA((2 * J,)),
                DMA((nc,)),
            ],
            input_output_aliases={5 + len(lefts): 0},
        )(rows, waves, mine, theirs, a_blocks, *lefts, start)

    if not plan.whole:
        a_pattern = lax.all_gather(a_pattern, "col", axis=1, tiled=True)
    b0 = plan.rows * plan.W
    entries = jnp.pad(b_pattern, ((0, plan.rows - 1), (b0, LANES - b0 - nc)))
    entries += jnp.pad(c_pattern, ((0, plan.rows - 1), (b0 + nc, LANES - b0 - 2 * nc)))
    entries += jnp.pad(a_pattern, ((0, 0), (0, LANES - plan.W)))

    b_pieces = b_blocks.reshape(nc, G, R, bs)
    width = plan.slots * bs + LANES
    pieces = call(
        functools.partial(prepare, plan),
        jax.ShapeDtypeStruct((G, R, width), F32),
        [VMEM, HBM],
        VMEM,
        [DMA((plan.slots,))],
    )(entries, b_pieces)
    got = exchange(pieces)
    lefts = []
    for wave in range(1 if plan.whole else plan.waves):
        staged = call(
            functools.partial(stage, plan, wave),
            (block,) * plan.ndep,
            [VMEM, HBM],
            (VMEM,) * plan.ndep,
            [DMA((plan.rows,))],
        )(entries, a_blocks)
        lefts += shift([staged[dd] for dd, _ in plan.others])

    tables = plan.tables()
    got, lefts = lax.optimization_barrier((got, lefts))
    rows, mine = listed(False, jnp.int32(0), got, got)
    late, waves, state, zero = settled(1, got, a_blocks)
    mine, late, zero = lax.optimization_barrier((mine, late, zero))
    lefts = lefts + late
    theirs = swap(mine)
    c_blocks = product(False, True, rows, waves, mine, theirs, a_blocks, lefts, zero)

    def rounds(raw, again, got, pieces, state, waves, a_blocks, lefts, begin, c_blocks):
        total = state[1] if plan.whole else lax.pmax(state[1], "col")

        def body(turn, c_blocks):
            rows, mine = listed(again, turn, got, pieces)
            return product(raw, False, rows, waves, mine, swap(mine), a_blocks, lefts, c_blocks)

        return lax.fori_loop(begin, total, body, c_blocks)

    def spread_again(b_pieces):
        return exchange(b_pieces.transpose(1, 2, 0, 3).reshape(G, R, nc * bs))

    def done(c_blocks, *_):
        return c_blocks

    def more_rounds(c_blocks, rows, mine, theirs, got, state, waves, a_blocks, b_pieces, *lefts):
        return rounds(False, False, got, got, state, waves, a_blocks, lefts, 1, c_blocks)

    def more_waves(c_blocks, rows, mine, theirs, got, state, waves, a_blocks, b_pieces, *lefts):
        lefts += tuple(settled(2, got, a_blocks)[0])
        return product(False, True, rows, waves, mine, theirs, a_blocks, lefts, c_blocks)

    def more_pieces(c_blocks, rows, mine, theirs, got, state, waves, a_blocks, b_pieces, *lefts):
        pieces, c_blocks = spread_again(b_pieces), jnp.zeros_like(c_blocks)
        return rounds(False, True, got, pieces, state, waves, a_blocks, lefts, 0, c_blocks)

    def anew(c_blocks, rows, mine, theirs, got, state, waves, a_blocks, b_pieces, *lefts):
        pieces, c_blocks = spread_again(b_pieces), jnp.zeros_like(c_blocks)
        dep = lax.axis_index("depth")
        raw = [lax.dynamic_index_in_dim(a_blocks, (dep + dd) % plan.ndep, keepdims=False) for dd, _ in plan.others]
        return rounds(True, True, got, pieces, state, waves, a_blocks, shift(raw), 0, c_blocks)

    index = state[0] if plan.whole else lax.pmax(state[0], "col")
    branches = [done, more_rounds, more_waves, more_pieces, anew]
    return lax.switch(index, branches, c_blocks, rows, mine, theirs, got, state, waves, a_blocks, b_pieces, *lefts)


def solution(mesh):
    in_specs = (
        P("row", ("depth", "col"), None, None),
        P("row", ("depth", "col")),
        P(("depth", "row"), "col", None, None),
        P(("depth", "row"), "col"),
        P(("row", "depth"), "col"),
    )
    out_specs = P(("row", "depth"), "col", None, None)
    return jax.shard_map(
        functools.partial(local, mesh), mesh=mesh, in_specs=in_specs, out_specs=out_specs, check_vma=False
    )
```

```python
import functools

import jax
import jax.numpy as jnp
import numpy as np
from jax import lax
from jax.experimental import pallas as pl
from jax.experimental.pallas import tpu as pltpu
from jax.sharding import PartitionSpec as P

LANES = 128
F32 = jnp.float32
BF16 = jnp.bfloat16
I32 = jnp.int32
SMEM = pl.BlockSpec(memory_space=pltpu.SMEM)
VMEM = pl.BlockSpec(memory_space=pltpu.VMEM)
HBM = pl.BlockSpec(memory_space=pltpu.HBM)
DMA = pltpu.SemaphoreType.DMA
PARAMS = pltpu.CompilerParams(vmem_limit_bytes=16 * 1024 * 1024)


class Plan:
    def __init__(self, mesh, a_blocks, b_blocks):
        self.nrow, self.ncol, self.ndep = (mesh.shape[name] for name in ("row", "col", "depth"))
        self.rows, self.kc, self.bs, _ = a_blocks.shape
        self.kb, self.nc, _, _ = b_blocks.shape
        assert self.kb == 1 and self.rows == self.ndep and self.nrow % 2 == 0
        every = self.nrow * self.ncol * self.ndep
        self.whole = self.bs // every >= 8
        self.axes = ("row", "col", "depth") if self.whole else ("row", "depth")
        self.G = every if self.whole else self.nrow * self.ndep
        self.stride = self.G // self.nrow
        self.R = self.bs // self.G
        self.Q = self.G * self.nc
        self.W = self.kc if self.whole else self.kc * self.ncol
        self.nk = self.kc * self.ncol * self.ndep
        self.J = 3 * self.nk // 16
        self.slots = self.nc - 1 if self.whole else self.nc
        self.waves = 2 if self.whole else self.kc
        assert self.G & (self.G - 1) == 0 and self.nc & (self.nc - 1) == 0
        self.g_bits, self.q_bits = self.G.bit_length() - 1, self.Q.bit_length() - 1
        self.others = [(dd, dc) for dd in range(self.ndep) for dc in range(self.ncol) if (dd, dc) != (0, 0)]

    def member(self, value):
        return (value >> 2) & (self.G - 1)

    def column(self, value):
        return (value >> (2 + self.g_bits)) & (self.nc - 1)

    def slot(self, value):
        return value >> (2 + self.q_bits)

    def listed(self, rows, p, member):
        per = LANES // self.G
        return rows[p // per, p % per * self.G + member]

    def decode(self, s):
        if self.whole:
            return s // (self.ncol * self.ndep), s // self.ndep % self.ncol, s % self.ndep
        return s // self.ndep, s * 0, s % self.ndep

    def tables(self, dtype=BF16):
        q = np.arange(self.Q)[None, :]
        s = np.arange(self.G)[:, None]
        e = np.arange(LANES)[:, None]
        row_q, col_q, dep_q = self.decode(q % self.G)
        c_q = q // self.G
        row_s, col_s, dep_s = self.decode(s)
        row_t, col_t, dep_t = self.decode(s.T)
        b0 = self.rows * self.W
        select = [e == rr * self.W + row_q % self.W for rr in range(self.rows)]
        select += [e == b0 + c_q, e == b0 + self.nc + c_q, (e >= b0) & (e < b0 + c_q)]
        holds = (dep_s == dep_q) & (col_s == row_q // self.W)
        masks = [holds, s == q % self.G, col_s == col_q]
        before = np.arange(self.Q)[:, None] < q
        k = np.arange(LANES)[None, :]
        inner = (dep_q * self.nrow + row_q).T == k
        first = inner & (c_q.T == 0) & (col_q.T == 0)
        chunk = (k.T < k) & (k.T // self.kc == k // self.kc) & (k < self.nk)
        pick = [(row_s == row_t) & (dep_s == rr) for rr in range(self.rows)]
        pick += [(row_s ^ 1 == row_t) & (col_s == col_t) & (dep_s == dep_t)]
        groups = [np.concatenate(select, 1), np.concatenate(masks, 0), before, np.concatenate(pick, 1)]
        far = (k // self.kc != dep_s * self.ncol + col_s) | (not self.whole)
        groups += [np.concatenate([inner, first], 1), np.concatenate([chunk, far], 0)]
        return [jnp.asarray(t.astype(np.float32), dtype) for t in groups]


def dot(x, y):
    return jnp.dot(x.astype(BF16), y.astype(BF16), preferred_element_type=F32)


def dot_high(x, y):
    x_high, y_high = x.astype(BF16), y.astype(BF16)
    x_low, y_low = (x - x_high.astype(F32)).astype(BF16), (y - y_high.astype(F32)).astype(BF16)
    x_terms = jnp.concatenate([x_high, x_low, x_high], axis=1)
    return dot(x_terms, jnp.concatenate([y_low, y_high, y_high], axis=0))


def entry_row(plan, entries):
    row = entries[0:1]
    for r in range(1, plan.rows):
        row += pltpu.roll(entries[r : r + 1], r * plan.W, 1)
    return row


def entry_bits(row, start, count):
    lane = lax.broadcasted_iota(I32, row.shape, 1) - start
    return jnp.sum(jnp.where((lane >= 0) & (lane < count), row << jnp.clip(lane, 0, count - 1), 0))


def prepare(plan, entries, b_hbm, out_hbm, blocks, tile_ref, sems, out_sems):
    def piece(c, j):
        return pltpu.make_async_copy(b_hbm.at[c], blocks.at[j], sems.at[j])

    def out(src, j, width):
        return pltpu.make_async_copy(src, out_hbm.at[:, :, pl.ds(j * plan.bs, width)], out_sems.at[j])

    row = entry_row(plan, entries)
    bits = entry_bits(row, plan.rows * plan.W, plan.nc)
    count = jnp.int32(0)
    for c in range(plan.nc):
        stored = (bits >> c) & 1 == 1
        for j in range(min(c + 1, plan.slots)):

            @pl.when(stored & (count == j))
            def _(c=c, j=j):
                piece(c, j).start()

        count += stored.astype(I32)

    tile_ref[...] = jnp.broadcast_to(row.astype(F32)[None], tile_ref.shape)
    last = out(tile_ref, plan.slots, LANES)
    last.start()
    for j in range(plan.slots):

        @pl.when(count > j)
        def _(j=j):
            piece(0, j).wait()
            out(blocks.at[j], j, plan.bs).start()

    last.wait()
    for j in range(plan.slots):

        @pl.when(count > j)
        def _(j=j):
            out(blocks.at[j], j, plan.bs).wait()


def stage(plan, wave, entries, a_hbm, *refs):
    outs, sems = refs[:-1], refs[-1]
    col, dep = lax.axis_index("col"), lax.axis_index("depth")
    row = entry_row(plan, entries)
    start = 0 if plan.whole else col * plan.kc
    bits = [entry_bits(row, r * plan.W + start, plan.kc) for r in range(plan.rows)]
    stored = [[(bits[r] >> kk) & 1 == 1 for kk in range(plan.kc)] for r in range(plan.rows)]

    def each(act):
        for r in range(plan.rows):
            count = jnp.int32(0)
            for kk in range(plan.kc):
                for dd, out in enumerate(outs):

                    @pl.when(stored[r][kk] & (count == wave) & ((dep + dd) % plan.ndep == r))
                    def _(r=r, kk=kk, out=out):
                        act(pltpu.make_async_copy(a_hbm.at[r, kk], out, sems.at[r]))

                count += stored[r][kk].astype(I32)

    each(lambda copy: copy.start())
    each(lambda copy: copy.wait())


def clear(plan, _, zero_hbm, zero, sems):
    zero[...] = jnp.zeros_like(zero)
    copies = [pltpu.make_async_copy(zero, zero_hbm.at[0, c], sems.at[c]) for c in range(plan.nc)]
    for copy in copies:
        copy.start()
    for copy in copies:
        copy.wait()


def needs(plan, tile, wide, masks, before, pick):
    G, Q, rows = plan.G, plan.Q, plan.rows
    entries = dot(tile, wide[...])
    holds, own, same_col = masks[0:G], masks[G : 2 * G], masks[2 * G : 3 * G]
    stored_a = jnp.zeros((G, Q), F32)
    for rr in range(rows):
        stored_a += dot(pick[:, rr * G : (rr + 1) * G], entries[:, rr * Q : (rr + 1) * Q] * holds)
    b0 = rows * Q
    stored_b = jnp.sum(entries[:, b0 : b0 + Q] * own, axis=0, keepdims=True)
    slot = jnp.sum(entries[:, b0 + 2 * Q : b0 + 3 * Q] * own, axis=0, keepdims=True)
    need = stored_a * stored_b * entries[:, b0 + Q : b0 + 2 * Q] * same_col
    partner = dot(pick[:, rows * G :], need)
    both = jnp.maximum(need, partner)
    return need, partner, both, dot(both, before[...]), slot, stored_a


def list_blocks(plan, base, need, partner, both, rank, slot, out):
    G, Q, per = plan.G, plan.Q, LANES // plan.G
    q = lax.broadcasted_iota(I32, (1, Q), 1).astype(F32)
    value = 4.0 * both * (slot * float(Q) + q) + 2.0 * partner + need
    member = lax.broadcasted_iota(I32, (G, LANES), 0)
    lane = lax.broadcasted_iota(I32, (G, LANES), 1)
    turn = rank - ((member[:, :1] >> (plan.stride.bit_length() - 1)) & 1).astype(F32) - base
    for n in range(out.shape[0]):
        row = jnp.zeros((G, LANES), F32)
        for p in range(n * per, min((n + 1) * per, plan.J)):
            at = jnp.sum(jnp.where(turn == 2.0 * p, value, 0.0), axis=1, keepdims=True)
            row = jnp.where(lane == p % per * G + member, at, row)
        out[n : n + 1] = jnp.sum(row, axis=0, keepdims=True).astype(I32)


def schedule(plan, turn, tile_ref, got_ref, *refs):
    tables, rest, refs = refs[:4], refs[4:-5], refs[-5:]
    out_ref, rows_ref, facts_ref, scratch, sem = refs
    base = 0.0 if turn is None else (turn[0] * (2 * plan.J)).astype(F32)
    need, partner, both, rank, slot, stored_a = needs(plan, tile_ref[:, 0, tile_ref.shape[2] - LANES :], *tables)
    list_blocks(plan, base, need, partner, both, rank, slot, rows_ref)
    copy = pltpu.make_async_copy(rows_ref, scratch, sem.at[0])
    copy.start()
    for n, fact in enumerate((need, both, stored_a, jnp.broadcast_to(slot, need.shape))):
        facts_ref[n] = fact
    copy.wait()
    for p in range(plan.J):

        def body(d, carry, p=p):
            value = plan.listed(scratch, p, d)
            slot = plan.slot(value)
            start = pl.multiple_of(jnp.minimum(slot, plan.slots - 1) * plan.bs, plan.bs)
            out_ref[d, p] = got_ref[plan.member(value), :, pl.ds(start, plan.bs)]
            if rest:

                @pl.when(slot >= plan.slots)
                def _():
                    out_ref[d, p] = rest[0][plan.member(value)]

            return carry

        lax.fori_loop(0, plan.G, body, 0, unroll=1 if rest else 8)


def settle(plan, wave, facts_ref, inner, chunk, a_hbm, *refs):
    outs, (waves_ref, state_ref, place_ref, place_smem, sems) = refs[:-5], refs[-5:]
    need, both, stored_a, slot = (facts_ref[n] for n in range(4))
    before, far = chunk[0:LANES], chunk[LANES:]
    left = jnp.minimum(dot(need, inner[:, :LANES]), 1.0)
    place = dot(dot(stored_a, inner[:, LANES:]), before)
    if plan.whole:
        late = jnp.where(place > 0, left, 0.0)
        place = jnp.where(place > 0, jnp.where(late > 0, 1.0 + dot(late, before), -1.0), 0.0)
    row, col, dep = lax.axis_index("row"), lax.axis_index("col"), lax.axis_index("depth")
    member = lax.broadcasted_iota(I32, place.shape, 0)
    owners = []
    for dd, dc in plan.others[: len(outs)]:
        to_dep, to_col = (dep + dd) % plan.ndep, (col + dc) % plan.ncol
        owners.append((to_dep, (row * plan.ncol + to_col) * plan.ndep + to_dep))
    for o, (_, to) in enumerate(owners):
        place_ref[o : o + 1] = jnp.sum(jnp.where(member == to, place, 0.0), axis=0, keepdims=True).astype(I32)
    fetch = pltpu.make_async_copy(place_ref, place_smem, sems.at[len(outs)])
    fetch.start()

    def each(act):
        for o, out in enumerate(outs):
            to_dep = owners[o][0]
            for kk in range(plan.kc):

                @pl.when(place_smem[o, dep * plan.nrow + col * plan.kc + kk] == wave)
                def _(o=o, kk=kk, out=out, to_dep=to_dep):
                    act(pltpu.make_async_copy(a_hbm.at[to_dep, kk], out, sems.at[o]))

    fetch.wait()
    each(lambda copy: copy.start())
    mine = jnp.where(member == lax.axis_index(plan.axes), place, 0.0)
    waves_ref[...] = jnp.sum(mine, axis=0, keepdims=True).astype(I32)
    rounds = (jnp.max(jnp.sum(both, axis=1, keepdims=True)).astype(I32) + 2 * plan.J - 1) // (2 * plan.J)
    lost = jnp.max(need * jnp.where(slot >= plan.slots, 1.0, 0.0)) > 0
    waves = jnp.max(left * far * (place + 1.0))
    easy = jnp.where(lost, 3, jnp.where(rounds > 1, 1, 0))
    hard = jnp.where((waves > plan.waves + 1) | lost, 4, 2)
    state_ref[0] = jnp.where(waves > plan.waves, hard, easy)
    state_ref[1] = rounds
    each(lambda copy: copy.wait())


def multiply(plan, raw, waves, first, rows, left, mine, theirs, a_hbm, *refs):
    lefts, refs = refs[: waves * len(plan.others)], refs[waves * len(plan.others) :]
    _, out_hbm, a_scr, total, sems, out_sems = refs
    col, dep = lax.axis_index("col"), lax.axis_index("depth")
    member = lax.axis_index(plan.axes)
    listed = [plan.listed(rows, p, member) for p in range(plan.J)]
    listed += [plan.listed(rows, p, member ^ plan.stride) >> 1 << 1 for p in range(plan.J)]
    asked = [value & 1 for value in listed[: plan.J]] + [(value >> 1) & 1 for value in listed[plan.J :]]

    def copy(src, j):
        return pltpu.make_async_copy(src, a_scr.at[j], sems.at[j])

    ready = []
    for j, value in enumerate(listed):
        row_s, _, dep_s = plan.decode(plan.member(value))
        dd = (dep - dep_s + plan.ndep) % plan.ndep
        dc = (col - row_s // plan.kc + plan.ncol) % plan.ncol
        kk = row_s % plan.kc
        near = (dd == 0) & (dc == 0)
        wave = jnp.int32(0) if raw else left[0, dep_s * plan.nrow + row_s]
        ready.append((asked[j] == 1) & (near | (wave < waves)))

        @pl.when(ready[j])
        def _(j=j, kk=kk, dd=dd, dc=dc, near=near, wave=wave):
            @pl.when(near)
            def _():
                copy(a_hbm.at[dep, kk], j).start()

            for n, (xd, xc) in enumerate(plan.others):
                for w in range(waves):

                    @pl.when((dd == xd) & (dc == xc) & (wave == w))
                    def _(n=n, w=w):
                        src = lefts[w * len(plan.others) + n]
                        copy(src.at[kk] if raw else src, j).start()

    def block(c):
        return pltpu.make_async_copy(total.at[c], out_hbm.at[0, c], out_sems.at[c])

    column = [plan.column(value) for value in listed]
    touched = [functools.reduce(jnp.logical_or, [r & (x == c) for r, x in zip(ready, column)]) for c in range(plan.nc)]
    for c in range(plan.nc):

        @pl.when(touched[c])
        def _(c=c):
            if first:
                total[c] = jnp.zeros((plan.bs, plan.bs), F32)
            else:
                begin = pltpu.make_async_copy(out_hbm.at[0, c], total.at[c], out_sems.at[c])
                begin.start()
                begin.wait()

    for j in range(2 * plan.J):

        @pl.when(ready[j])
        def _(j=j):
            source = mine if j < plan.J else theirs
            right = source[:, j % plan.J].reshape(plan.bs, plan.bs)
            copy(a_hbm.at[0, 0], j).wait()
            total[column[j]] += dot_high(a_scr[j], right)

    for act in (lambda copy: copy.start(), lambda copy: copy.wait()):
        for c in range(plan.nc):
            pl.when(touched[c])(lambda c=c, act=act: act(block(c)))


def call(kernel, out_shape, in_specs, out_specs, scratch=(), **kwargs):
    return pl.pallas_call(
        kernel,
        out_shape=out_shape,
        in_specs=in_specs,
        out_specs=out_specs,
        scratch_shapes=scratch,
        compiler_params=PARAMS,
        name=kernel.func.__name__,
        **kwargs,
    )


def local(mesh, a_blocks, a_pattern, b_blocks, b_pattern, c_pattern):
    plan = Plan(mesh, a_blocks, b_blocks)
    G, R, J, bs, nc = plan.G, plan.R, plan.J, plan.bs, plan.nc
    result = jax.ShapeDtypeStruct((1, nc, bs, bs), F32)
    block = jax.ShapeDtypeStruct((bs, bs), F32)
    listing = (-(-J * G // LANES), LANES)

    def exchange(pieces):
        return lax.all_to_all(pieces, plan.axes, 0, 0, tiled=True)

    def shift(staged):
        def perm(dd, dc):
            for x in range(plan.ncol):
                for y in range(plan.ndep):
                    yield x * plan.ndep + y, (x + dc) % plan.ncol * plan.ndep + (y + dd) % plan.ndep

        return [lax.ppermute(x, ("col", "depth"), list(perm(*by))) for x, by in zip(staged, plan.others)]

    def swap(mine):
        return lax.ppermute(mine, "row", [(i, i ^ 1) for i in range(plan.nrow)])

    def listed(turn, got, rest, tables):
        first = turn is None
        return call(
            functools.partial(schedule, plan, *(None,) * first),
            (
                jax.ShapeDtypeStruct((G, J, R, bs), F32),
                jax.ShapeDtypeStruct(listing, I32),
                jax.ShapeDtypeStruct((4, G, plan.Q), F32),
            ),
            [SMEM] * (not first) + [VMEM] * (6 + len(rest)),
            (VMEM, VMEM, VMEM),
            [pltpu.SMEM(listing, I32), DMA((1,))],
        )(*[] if first else [jnp.reshape(turn, (1,))], got, got, *tables[:4], *rest)

    def settled(wave, facts, a_blocks, tables):
        count = len(plan.others) if plan.whole else 0
        *sent, waves, state = call(
            functools.partial(settle, plan, wave),
            (block,) * count + (jax.ShapeDtypeStruct((1, LANES), I32), jax.ShapeDtypeStruct((2,), I32)),
            [VMEM] * 3 + [HBM],
            (VMEM,) * count + (VMEM, SMEM),
            [pltpu.VMEM((8, LANES), I32), pltpu.SMEM((8, LANES), I32), DMA((count + 1,))],
        )(facts, *tables[4:], a_blocks)
        return shift(sent), waves, state

    def product(raw, first, rows, waves, mine, theirs, a_blocks, lefts, start):
        return call(
            functools.partial(multiply, plan, raw, len(lefts) // len(plan.others), first),
            result,
            [SMEM, SMEM, VMEM, VMEM] + [HBM] * (2 + len(lefts)),
            HBM,
            [
                pltpu.VMEM((2 * J, bs, bs), F32),
                pltpu.VMEM((nc, bs, bs), F32),
                DMA((2 * J,)),
                DMA((nc,)),
            ],
            input_output_aliases={5 + len(lefts): 0},
        )(rows, waves, mine, theirs, a_blocks, *lefts, start)

    if not plan.whole:
        a_pattern = lax.all_gather(a_pattern, "col", axis=1, tiled=True)
    b0 = plan.rows * plan.W
    entries = jnp.pad(b_pattern, ((0, plan.rows - 1), (b0, LANES - b0 - nc)))
    entries += jnp.pad(c_pattern, ((0, plan.rows - 1), (b0 + nc, LANES - b0 - 2 * nc)))
    entries += jnp.pad(a_pattern, ((0, 0), (0, LANES - plan.W)))

    b_pieces = b_blocks.reshape(nc, G, R, bs)
    width = plan.slots * bs + LANES
    pieces = call(
        functools.partial(prepare, plan),
        jax.ShapeDtypeStruct((G, R, width), F32),
        [VMEM, HBM],
        HBM,
        [
            pltpu.VMEM((plan.slots, G, R, bs), F32),
            pltpu.VMEM((G, R, LANES), F32),
            DMA((plan.slots,)),
            DMA((plan.slots + 1,)),
        ],
    )(entries, b_pieces)
    got = exchange(pieces)
    lefts = []
    for wave in range(1 if plan.whole else plan.waves):
        staged = call(
            functools.partial(stage, plan, wave),
            (block,) * plan.ndep,
            [VMEM, HBM],
            (VMEM,) * plan.ndep,
            [DMA((plan.rows,))],
        )(entries, a_blocks)
        lefts += shift([staged[dd] for dd, _ in plan.others])

    tables = plan.tables()
    zero = call(
        functools.partial(clear, plan), result, [VMEM], HBM, [pltpu.VMEM((bs, bs), F32), DMA((nc,))]
    )(staged[0])
    got, lefts, zero = lax.optimization_barrier((got, lefts, zero))
    send, rows, facts = listed(None, got, [], tables)
    mine = exchange(send)
    sent, waves, state = settled(1, facts, a_blocks, tables)
    mine, sent = lax.optimization_barrier((mine, sent))
    lefts = lefts + sent
    theirs = swap(mine)
    c_blocks = product(False, True, rows, waves, mine, theirs, a_blocks, lefts, zero)

    again = plan.tables(F32)

    def rounds(raw, rest, got, state, waves, a_blocks, lefts, begin, c_blocks):
        total = state[1] if plan.whole else lax.pmax(state[1], "col")

        def body(turn, c_blocks):
            send, rows, _ = listed(turn, got, rest, again)
            mine = exchange(send)
            return product(raw, False, rows, waves, mine, swap(mine), a_blocks, lefts, c_blocks)

        return lax.fori_loop(begin, total, body, c_blocks)

    def spread_rest(b_pieces):
        return [exchange(b_pieces[plan.slots])] if plan.slots < nc else []

    def done(c_blocks, *_):
        return c_blocks

    def more_rounds(c_blocks, rows, mine, theirs, got, facts, state, waves, a_blocks, b_pieces, *lefts):
        return rounds(False, [], got, state, waves, a_blocks, lefts, 1, c_blocks)

    def more_waves(c_blocks, rows, mine, theirs, got, facts, state, waves, a_blocks, b_pieces, *lefts):
        lefts += tuple(settled(2, facts, a_blocks, again)[0])
        c_blocks = product(False, True, rows, waves, mine, theirs, a_blocks, lefts, c_blocks)
        return rounds(False, [], got, state, waves, a_blocks, lefts, 1, c_blocks)

    def more_pieces(c_blocks, rows, mine, theirs, got, facts, state, waves, a_blocks, b_pieces, *lefts):
        c_blocks = jnp.zeros_like(c_blocks)
        return rounds(False, spread_rest(b_pieces), got, state, waves, a_blocks, lefts, 0, c_blocks)

    def anew(c_blocks, rows, mine, theirs, got, facts, state, waves, a_blocks, b_pieces, *lefts):
        c_blocks = jnp.zeros_like(c_blocks)
        dep = lax.axis_index("depth")
        raw = [lax.dynamic_index_in_dim(a_blocks, (dep + dd) % plan.ndep, keepdims=False) for dd, _ in plan.others]
        return rounds(True, spread_rest(b_pieces), got, state, waves, a_blocks, shift(raw), 0, c_blocks)

    index = state[0] if plan.whole else lax.pmax(state[0], "col")
    branches = [done, more_rounds, more_waves, more_pieces, anew]
    kept = (rows, mine, theirs, got, facts, state, waves, a_blocks, b_pieces)
    return lax.switch(index, branches, c_blocks, *kept, *lefts)


def solution(mesh):
    in_specs = (
        P("row", ("depth", "col"), None, None),
        P("row", ("depth", "col")),
        P(("depth", "row"), "col", None, None),
        P(("depth", "row"), "col"),
        P(("row", "depth"), "col"),
    )
    out_specs = P(("row", "depth"), "col", None, None)
    return jax.shard_map(
        functools.partial(local, mesh), mesh=mesh, in_specs=in_specs, out_specs=out_specs, check_vma=False
    )
```

```python
import functools

import jax
import jax.numpy as jnp
import numpy as np
from jax import lax
from jax.experimental import pallas as pl
from jax.experimental.pallas import tpu as pltpu
from jax.sharding import PartitionSpec as P

LANES = 128
PARTS = 4
F32 = jnp.float32
BF16 = jnp.bfloat16
I32 = jnp.int32
SMEM = pl.BlockSpec(memory_space=pltpu.SMEM)
VMEM = pl.BlockSpec(memory_space=pltpu.VMEM)
HBM = pl.BlockSpec(memory_space=pltpu.HBM)
DMA = pltpu.SemaphoreType.DMA
PARAMS = pltpu.CompilerParams(vmem_limit_bytes=16 * 1024 * 1024)


class Plan:
    def __init__(self, mesh, a_blocks, b_blocks):
        self.nrow, self.ncol, self.ndep = (mesh.shape[name] for name in ("row", "col", "depth"))
        self.rows, self.kc, self.bs, _ = a_blocks.shape
        self.kb, self.nc, _, _ = b_blocks.shape
        assert self.kb == 1 and self.rows == self.ndep and self.nrow % 2 == 0
        every = self.nrow * self.ncol * self.ndep
        self.whole = self.bs // every >= 8
        self.axes = ("row", "col", "depth") if self.whole else ("row", "depth")
        self.G = every if self.whole else self.nrow * self.ndep
        self.stride = self.G // self.nrow
        self.R = self.bs // self.G
        self.Q = self.G * self.nc
        self.W = self.kc if self.whole else self.kc * self.ncol
        self.nk = self.kc * self.ncol * self.ndep
        self.J = 3 * self.nk // 16
        self.more = self.nk // 16
        self.slots = self.nc - 1 if self.whole else self.nc
        self.waves = 2 if self.whole else self.kc
        assert self.G & (self.G - 1) == 0 and self.nc & (self.nc - 1) == 0
        self.g_bits, self.q_bits = self.G.bit_length() - 1, self.Q.bit_length() - 1
        self.others = [(dd, dc) for dd in range(self.ndep) for dc in range(self.ncol) if (dd, dc) != (0, 0)]

    def member(self, value):
        return (value >> 2) & (self.G - 1)

    def column(self, value):
        return (value >> (2 + self.g_bits)) & (self.nc - 1)

    def slot(self, value):
        return value >> (2 + self.q_bits)

    def listed(self, rows, p, member):
        per = LANES // self.G
        return rows[p // per, p % per * self.G + member]

    def decode(self, s):
        if self.whole:
            return s // (self.ncol * self.ndep), s // self.ndep % self.ncol, s % self.ndep
        return s // self.ndep, s * 0, s % self.ndep

    def tables(self, dtype=BF16):
        q = np.arange(self.Q)[None, :]
        s = np.arange(self.G)[:, None]
        e = np.arange(LANES)[:, None]
        row_q, col_q, dep_q = self.decode(q % self.G)
        c_q = q // self.G
        row_s, col_s, dep_s = self.decode(s)
        row_t, col_t, dep_t = self.decode(s.T)
        b0 = self.rows * self.W
        select = [e == rr * self.W + row_q % self.W for rr in range(self.rows)]
        select += [e == b0 + c_q, e == b0 + self.nc + c_q, (e >= b0) & (e < b0 + c_q)]
        holds = (dep_s == dep_q) & (col_s == row_q // self.W)
        masks = [holds, s == q % self.G, col_s == col_q]
        before = np.arange(self.Q)[:, None] < q
        k = np.arange(LANES)[None, :]
        inner = (dep_q * self.nrow + row_q).T == k
        first = inner & (c_q.T == 0) & (col_q.T == 0)
        chunk = (k.T < k) & (k.T // self.kc == k // self.kc) & (k < self.nk)
        pick = [(row_s == row_t) & (dep_s == rr) for rr in range(self.rows)]
        pick += [(row_s ^ 1 == row_t) & (col_s == col_t) & (dep_s == dep_t)]
        groups = [np.concatenate(select, 1), np.concatenate(masks, 0), before, np.concatenate(pick, 1)]
        dd = (dep_s - k // self.kc // self.ncol) % self.ndep
        dc = (col_s - k // self.kc % self.ncol) % self.ncol
        away = (dd * self.ncol + dc if self.whole else np.ones_like(dd)) * (k < self.nk)
        groups += [np.concatenate([inner, first], 1), np.concatenate([chunk, away], 0)]
        return [jnp.asarray(t.astype(np.float32), dtype) for t in groups]


def dot(x, y):
    return jnp.dot(x.astype(BF16), y.astype(BF16), preferred_element_type=F32)


def dot_high(x, y):
    x_high, y_high = x.astype(BF16), y.astype(BF16)
    x_low, y_low = (x - x_high.astype(F32)).astype(BF16), (y - y_high.astype(F32)).astype(BF16)
    x_terms = jnp.concatenate([x_high, x_low, x_high], axis=1)
    return dot(x_terms, jnp.concatenate([y_low, y_high, y_high], axis=0))


def entry_row(plan, entries):
    row = entries[0:1]
    for r in range(1, plan.rows):
        row += pltpu.roll(entries[r : r + 1], r * plan.W, 1)
    return row


def entry_bits(row, start, count):
    lane = lax.broadcasted_iota(I32, row.shape, 1) - start
    return jnp.sum(jnp.where((lane >= 0) & (lane < count), row << jnp.clip(lane, 0, count - 1), 0))


def prepare(plan, entries, b_hbm, out_hbm, blocks, tile_ref, sems, out_sems):
    def piece(c, j):
        return pltpu.make_async_copy(b_hbm.at[c], blocks.at[j], sems.at[j])

    def out(src, j, width):
        return pltpu.make_async_copy(src, out_hbm.at[:, :, pl.ds(j * plan.bs, width)], out_sems.at[j])

    row = entry_row(plan, entries)
    bits = entry_bits(row, plan.rows * plan.W, plan.nc)
    count = jnp.int32(0)
    for c in range(plan.nc):
        stored = (bits >> c) & 1 == 1
        for j in range(min(c + 1, plan.slots)):

            @pl.when(stored & (count == j))
            def _(c=c, j=j):
                piece(c, j).start()

        count += stored.astype(I32)

    tile_ref[...] = jnp.broadcast_to(row.astype(F32)[None], tile_ref.shape)
    last = out(tile_ref, plan.slots, LANES)
    last.start()
    for j in range(plan.slots):

        @pl.when(count > j)
        def _(j=j):
            piece(0, j).wait()
            out(blocks.at[j], j, plan.bs).start()

    last.wait()
    for j in range(plan.slots):

        @pl.when(count > j)
        def _(j=j):
            out(blocks.at[j], j, plan.bs).wait()


def stage(plan, wave, entries, a_hbm, *refs):
    outs, sems = refs[:-1], refs[-1]
    col, dep = lax.axis_index("col"), lax.axis_index("depth")
    row = entry_row(plan, entries)
    start = 0 if plan.whole else col * plan.kc
    bits = [entry_bits(row, r * plan.W + start, plan.kc) for r in range(plan.rows)]
    stored = [[(bits[r] >> kk) & 1 == 1 for kk in range(plan.kc)] for r in range(plan.rows)]

    def each(act):
        for r in range(plan.rows):
            count = jnp.int32(0)
            for kk in range(plan.kc):
                for dd, out in enumerate(outs):

                    @pl.when(stored[r][kk] & (count == wave) & ((dep + dd) % plan.ndep == r))
                    def _(r=r, kk=kk, out=out):
                        act(pltpu.make_async_copy(a_hbm.at[r, kk], out, sems.at[r]))

                count += stored[r][kk].astype(I32)

    each(lambda copy: copy.start())
    each(lambda copy: copy.wait())


def clear(plan, _, zero_hbm, zero, sems):
    zero[...] = jnp.zeros_like(zero)
    copies = [pltpu.make_async_copy(zero, zero_hbm.at[0, c], sems.at[c]) for c in range(plan.nc)]
    for copy in copies:
        copy.start()
    for copy in copies:
        copy.wait()


def needs(plan, tile, wide, masks, before, pick):
    G, Q, rows = plan.G, plan.Q, plan.rows
    entries = dot(tile, wide[...])
    holds, own, same_col = masks[0:G], masks[G : 2 * G], masks[2 * G : 3 * G]
    stored_a = jnp.zeros((G, Q), F32)
    for rr in range(rows):
        stored_a += dot(pick[:, rr * G : (rr + 1) * G], entries[:, rr * Q : (rr + 1) * Q] * holds)
    b0 = rows * Q
    stored_b = jnp.sum(entries[:, b0 : b0 + Q] * own, axis=0, keepdims=True)
    slot = jnp.sum(entries[:, b0 + 2 * Q : b0 + 3 * Q] * own, axis=0, keepdims=True)
    need = stored_a * stored_b * entries[:, b0 + Q : b0 + 2 * Q] * same_col
    partner = dot(pick[:, rows * G :], need)
    both = jnp.maximum(need, partner)
    return need, partner, both, dot(both, before[...]), slot, stored_a


def list_blocks(plan, J, base, need, partner, both, rank, slot, out):
    G, Q, per = plan.G, plan.Q, LANES // plan.G
    q = lax.broadcasted_iota(I32, (1, Q), 1).astype(F32)
    value = 4.0 * both * (slot * float(Q) + q) + 2.0 * partner + need
    member = lax.broadcasted_iota(I32, (G, LANES), 0)
    lane = lax.broadcasted_iota(I32, (G, LANES), 1)
    turn = rank - ((member[:, :1] >> (plan.stride.bit_length() - 1)) & 1).astype(F32) - base
    for n in range(out.shape[0]):
        row = jnp.zeros((G, LANES), F32)
        for p in range(n * per, min((n + 1) * per, J)):
            at = jnp.sum(jnp.where(turn == 2.0 * p, value, 0.0), axis=1, keepdims=True)
            row = jnp.where(lane == p % per * G + member, at, row)
        out[n : n + 1] = jnp.sum(row, axis=0, keepdims=True).astype(I32)


def schedule(plan, J, base, tile_ref, got_ref, *refs):
    tables, rest, refs = refs[:4], refs[4:-7], refs[-7:]
    out_hbm, rows_ref, facts_ref, pieces, scratch, sem, out_sems = refs
    start = 0.0 if base is None else base[0].astype(F32)
    need, partner, both, rank, slot, stored_a = needs(plan, tile_ref[:, 0, tile_ref.shape[2] - LANES :], *tables)
    list_blocks(plan, J, start, need, partner, both, rank, slot, rows_ref)
    copy = pltpu.make_async_copy(rows_ref, scratch, sem.at[0])
    copy.start()
    for n, fact in enumerate((need, both, stored_a, jnp.broadcast_to(slot, need.shape))):
        facts_ref[n] = fact
    copy.wait()

    def take(d):
        for p in range(J):
            value = plan.listed(scratch, p, d)
            slot = plan.slot(value)
            lane = pl.multiple_of(jnp.minimum(slot, plan.slots - 1) * plan.bs, plan.bs)
            pieces[d, p] = got_ref[plan.member(value), :, pl.ds(lane, plan.bs)]
            if rest:

                @pl.when(slot >= plan.slots)
                def _():
                    pieces[d, p] = rest[0][plan.member(value)]

    size = plan.G // PARTS
    copies = []
    for n in range(PARTS):
        part = pl.ds(n * size, size)
        copies.append(pltpu.make_async_copy(pieces.at[part], out_hbm.at[part], out_sems.at[n]))

        @pl.loop(n * size, (n + 1) * size, unroll=1 if rest else size)
        def _(d):
            take(d)

        copies[n].start()
    for copy in copies:
        copy.wait()


def settle(plan, wave, facts_ref, rows_ref, inner, chunk, a_hbm, *refs):
    outs, refs = refs[:-7], refs[-7:]
    waves_ref, waves_again, rows_again, state_ref, place_ref, place_smem, sems = refs
    rows_again[...] = rows_ref[...]
    need, both, stored_a, slot = (facts_ref[n] for n in range(4))
    before, away = chunk[0:LANES], chunk[LANES:].astype(F32)
    left = jnp.minimum(dot(need, inner[:, :LANES]), 1.0)
    place = dot(dot(stored_a, inner[:, LANES:]), before)
    if plan.whole:
        late = jnp.where(place > 0, left, 0.0)
        place = jnp.where(place > 0, jnp.where(late > 0, 1.0 + dot(late, before), -1.0), 0.0)
    row, col, dep = lax.axis_index("row"), lax.axis_index("col"), lax.axis_index("depth")
    member = lax.broadcasted_iota(I32, place.shape, 0)
    owners = []
    for dd, dc in plan.others[: len(outs)]:
        to_dep, to_col = (dep + dd) % plan.ndep, (col + dc) % plan.ncol
        owners.append((to_dep, (row * plan.ncol + to_col) * plan.ndep + to_dep))
    for o, (_, to) in enumerate(owners):
        place_ref[o : o + 1] = jnp.sum(jnp.where(member == to, place, 0.0), axis=0, keepdims=True).astype(I32)
    fetch = pltpu.make_async_copy(place_ref, place_smem, sems.at[len(outs)])
    fetch.start()

    def each(act):
        for o, out in enumerate(outs):
            to_dep = owners[o][0]
            for kk in range(plan.kc):

                @pl.when(place_smem[o, dep * plan.nrow + col * plan.kc + kk] == wave)
                def _(o=o, kk=kk, out=out, to_dep=to_dep):
                    act(pltpu.make_async_copy(a_hbm.at[to_dep, kk], out, sems.at[o]))

    fetch.wait()
    each(lambda copy: copy.start())
    mine = jnp.where(member == lax.axis_index(plan.axes), place, 0.0)
    waves_ref[...] = jnp.sum(mine, axis=0, keepdims=True).astype(I32)
    waves_again[...] = waves_ref[...]
    most = jnp.max(jnp.sum(both, axis=1, keepdims=True)).astype(I32)
    lost = jnp.max(need * jnp.where(slot >= plan.slots, 1.0, 0.0)) > 0
    waves = jnp.max(left * jnp.where(away > 0, 1.0, 0.0) * (place + 1.0))
    last = left * jnp.where(place == float(plan.waves), 1.0, 0.0) * away
    count = len(plan.others) if plan.whole else 0
    way = jnp.int32(2 + count)
    for o in range(count):
        way = jnp.where(jnp.max(jnp.where(last == o + 1.0, 0.0, last)) == 0.0, 2 + o, way)
    easy = jnp.where(lost, 3 + count, jnp.where(most > 2 * plan.J, 1, 0))
    hard = jnp.where((waves > plan.waves + 1) | lost, 4 + count, way)
    state_ref[0] = jnp.where(waves > plan.waves, hard, easy)
    state_ref[1] = most
    each(lambda copy: copy.wait())


def multiply(plan, J, raw, waves, first, rows, left, mine, theirs, a_hbm, *refs):
    lefts, refs = refs[: waves * len(plan.others)], refs[waves * len(plan.others) :]
    _, out_hbm, a_scr, total, sems, out_sems = refs
    col, dep = lax.axis_index("col"), lax.axis_index("depth")
    member = lax.axis_index(plan.axes)
    listed = [plan.listed(rows, p, member) for p in range(J)]
    listed += [plan.listed(rows, p, member ^ plan.stride) >> 1 << 1 for p in range(J)]
    asked = [value & 1 for value in listed[: J]] + [(value >> 1) & 1 for value in listed[J :]]

    def copy(src, j):
        return pltpu.make_async_copy(src, a_scr.at[j], sems.at[j])

    ready = []
    for j, value in enumerate(listed):
        row_s, _, dep_s = plan.decode(plan.member(value))
        dd = (dep - dep_s + plan.ndep) % plan.ndep
        dc = (col - row_s // plan.kc + plan.ncol) % plan.ncol
        kk = row_s % plan.kc
        near = (dd == 0) & (dc == 0)
        wave = jnp.int32(0) if raw else left[0, dep_s * plan.nrow + row_s]
        ready.append((asked[j] == 1) & (near | (wave < waves)))

        @pl.when(ready[j])
        def _(j=j, kk=kk, dd=dd, dc=dc, near=near, wave=wave):
            @pl.when(near)
            def _():
                copy(a_hbm.at[dep, kk], j).start()

            for n, (xd, xc) in enumerate(plan.others):
                for w in range(waves):

                    @pl.when((dd == xd) & (dc == xc) & (wave == w))
                    def _(n=n, w=w):
                        src = lefts[w * len(plan.others) + n]
                        copy(src.at[kk] if raw else src, j).start()

    def block(c):
        return pltpu.make_async_copy(total.at[c], out_hbm.at[0, c], out_sems.at[c])

    column = [plan.column(value) for value in listed]
    touched = [functools.reduce(jnp.logical_or, [r & (x == c) for r, x in zip(ready, column)]) for c in range(plan.nc)]
    for c in range(plan.nc):

        @pl.when(touched[c])
        def _(c=c):
            if first:
                total[c] = jnp.zeros((plan.bs, plan.bs), F32)
            else:
                begin = pltpu.make_async_copy(out_hbm.at[0, c], total.at[c], out_sems.at[c])
                begin.start()
                begin.wait()

    for j in range(2 * J):

        @pl.when(ready[j])
        def _(j=j):
            source = mine if j < J else theirs
            right = source[:, j % J].reshape(plan.bs, plan.bs)
            copy(a_hbm.at[0, 0], j).wait()
            total[column[j]] += dot_high(a_scr[j], right)

    for act in (lambda copy: copy.start(), lambda copy: copy.wait()):
        for c in range(plan.nc):
            pl.when(touched[c])(lambda c=c, act=act: act(block(c)))


def call(kernel, out_shape, in_specs, out_specs, scratch=(), **kwargs):
    return pl.pallas_call(
        kernel,
        out_shape=out_shape,
        in_specs=in_specs,
        out_specs=out_specs,
        scratch_shapes=scratch,
        compiler_params=PARAMS,
        name=kernel.func.__name__,
        **kwargs,
    )


def local(mesh, a_blocks, a_pattern, b_blocks, b_pattern, c_pattern):
    plan = Plan(mesh, a_blocks, b_blocks)
    G, R, J, bs, nc = plan.G, plan.R, plan.J, plan.bs, plan.nc
    result = jax.ShapeDtypeStruct((1, nc, bs, bs), F32)
    block = jax.ShapeDtypeStruct((bs, bs), F32)

    def exchange(pieces):
        return lax.all_to_all(pieces, plan.axes, 0, 0, tiled=True)

    def shift(staged, only=None):
        def perm(dd, dc):
            for x in range(plan.ncol):
                for y in range(plan.ndep):
                    yield x * plan.ndep + y, (x + dc) % plan.ncol * plan.ndep + (y + dd) % plan.ndep

        names = range(len(staged)) if only is None else only
        return [lax.ppermute(staged[o], ("col", "depth"), list(perm(*plan.others[o]))) for o in names]

    def swap(mine):
        return lax.ppermute(mine, "row", [(i, i ^ 1) for i in range(plan.nrow)])

    def listed(J, base, got, rest, tables):
        first = base is None
        listing = (-(-J * G // LANES), LANES)
        return call(
            functools.partial(schedule, plan, J, *(None,) * first),
            (
                jax.ShapeDtypeStruct((G, J, R, bs), F32),
                jax.ShapeDtypeStruct(listing, I32),
                jax.ShapeDtypeStruct((4, G, plan.Q), F32),
            ),
            [SMEM] * (not first) + [VMEM] * (6 + len(rest)),
            (HBM, VMEM, VMEM),
            [pltpu.VMEM((G, J, R, bs), F32), pltpu.SMEM(listing, I32), DMA((1,)), DMA((PARTS,))],
        )(*[] if first else [jnp.reshape(base, (1,))], got, got, *tables[:4], *rest)

    def settled(wave, facts, rows, a_blocks, tables):
        count = len(plan.others) if plan.whole else 0
        line, lists = jax.ShapeDtypeStruct((1, LANES), I32), jax.ShapeDtypeStruct(rows.shape, I32)
        *sent, waves, waves_again, rows_again, state = call(
            functools.partial(settle, plan, wave),
            (block,) * count + (line, line, lists, jax.ShapeDtypeStruct((2,), I32)),
            [VMEM] * 4 + [HBM],
            (VMEM,) * count + (VMEM, VMEM, VMEM, SMEM),
            [pltpu.VMEM((8, LANES), I32), pltpu.SMEM((8, LANES), I32), DMA((count + 1,))],
        )(facts, rows, *tables[4:], a_blocks)
        return sent, waves, waves_again, rows_again, state

    def product(J, raw, first, rows, waves, mine, theirs, a_blocks, lefts, start):
        return call(
            functools.partial(multiply, plan, J, raw, len(lefts) // len(plan.others), first),
            result,
            [SMEM, SMEM, VMEM, VMEM] + [HBM] * (2 + len(lefts)),
            HBM,
            [
                pltpu.VMEM((2 * J, bs, bs), F32),
                pltpu.VMEM((nc, bs, bs), F32),
                DMA((2 * J,)),
                DMA((nc,)),
            ],
            input_output_aliases={5 + len(lefts): 0},
        )(rows, waves, mine, theirs, a_blocks, *lefts, start)

    if not plan.whole:
        a_pattern = lax.all_gather(a_pattern, "col", axis=1, tiled=True)
    b0 = plan.rows * plan.W
    entries = jnp.pad(b_pattern, ((0, plan.rows - 1), (b0, LANES - b0 - nc)))
    entries += jnp.pad(c_pattern, ((0, plan.rows - 1), (b0 + nc, LANES - b0 - 2 * nc)))
    entries += jnp.pad(a_pattern, ((0, 0), (0, LANES - plan.W)))

    b_pieces = b_blocks.reshape(nc, G, R, bs)
    width = plan.slots * bs + LANES
    pieces = call(
        functools.partial(prepare, plan),
        jax.ShapeDtypeStruct((G, R, width), F32),
        [VMEM, HBM],
        HBM,
        [
            pltpu.VMEM((plan.slots, G, R, bs), F32),
            pltpu.VMEM((G, R, LANES), F32),
            DMA((plan.slots,)),
            DMA((plan.slots + 1,)),
        ],
    )(entries, b_pieces)
    got = exchange(pieces)
    lefts = []
    for wave in range(1 if plan.whole else plan.waves):
        staged = call(
            functools.partial(stage, plan, wave),
            (block,) * plan.ndep,
            [VMEM, HBM],
            (VMEM,) * plan.ndep,
            [DMA((plan.rows,))],
        )(entries, a_blocks)
        lefts += shift([staged[dd] for dd, _ in plan.others])

    tables = plan.tables()
    zero = call(
        functools.partial(clear, plan), result, [VMEM], HBM, [pltpu.VMEM((bs, bs), F32), DMA((nc,))]
    )(staged[0])
    got, lefts, zero = lax.optimization_barrier((got, lefts, zero))
    send, rows, facts = listed(J, None, got, [], tables)
    mine = exchange(send)
    sent, waves, waves_again, rows_again, state = settled(1, facts, rows, a_blocks, tables)
    sent = shift(sent)
    mine, sent = lax.optimization_barrier((mine, sent))
    lefts = lefts + sent
    theirs = swap(mine)
    near = [pltpu.with_memory_space_constraint(x, pltpu.VMEM) for x in (mine, theirs)]
    c_blocks = product(J, False, True, rows, waves, *near, a_blocks, lefts, zero)

    again = plan.tables(F32)

    def rounds(J, begin, raw, rest, got, state, waves, a_blocks, lefts, c_blocks):
        most = state[1] if plan.whole else lax.pmax(state[1], "col")

        def body(turn, c_blocks):
            send, rows, _ = listed(J, begin + 2 * J * turn, got, rest, again)
            mine = exchange(send)
            return product(J, raw, False, rows, waves, mine, swap(mine), a_blocks, lefts, c_blocks)

        return lax.fori_loop(0, (jnp.maximum(most - begin, 0) + 2 * J - 1) // (2 * J), body, c_blocks)

    def spread_rest(b_pieces):
        return [exchange(b_pieces[plan.slots])] if plan.slots < nc else []

    def done(c_blocks, *_):
        return c_blocks

    def more_rounds(c_blocks, rows, mine, theirs, got, facts, state, waves, a_blocks, b_pieces, *lefts):
        return rounds(plan.more, 2 * J, False, [], got, state, waves, a_blocks, lefts, c_blocks)

    def more_waves(way, c_blocks, rows, mine, theirs, got, facts, state, waves, a_blocks, b_pieces, *lefts):
        sent = settled(2, facts, rows, a_blocks, again)[0]
        for o in range(len(sent)):
            if way in (o, len(sent)):
                sent[o] = shift(sent, [o])[0]
        c_blocks = product(J, False, True, rows, waves, mine, theirs, a_blocks, lefts + tuple(sent), c_blocks)
        return rounds(plan.more, 2 * J, False, [], got, state, waves, a_blocks, lefts + tuple(sent), c_blocks)

    def more_pieces(c_blocks, rows, mine, theirs, got, facts, state, waves, a_blocks, b_pieces, *lefts):
        c_blocks = jnp.zeros_like(c_blocks)
        return rounds(J, 0, False, spread_rest(b_pieces), got, state, waves, a_blocks, lefts, c_blocks)

    def anew(c_blocks, rows, mine, theirs, got, facts, state, waves, a_blocks, b_pieces, *lefts):
        c_blocks = jnp.zeros_like(c_blocks)
        dep = lax.axis_index("depth")
        raw = [lax.dynamic_index_in_dim(a_blocks, (dep + dd) % plan.ndep, keepdims=False) for dd, _ in plan.others]
        return rounds(J, 0, True, spread_rest(b_pieces), got, state, waves, a_blocks, shift(raw), c_blocks)

    index = state[0] if plan.whole else lax.pmax(state[0], "col")
    ways = [functools.partial(more_waves, way) for way in range(len(plan.others) * plan.whole + 1)]
    branches = [done, more_rounds, *ways, more_pieces, anew]
    kept = (rows_again, mine, theirs, got, facts, state, waves_again, a_blocks, b_pieces)
    return lax.switch(index, branches, c_blocks, *kept, *lefts)


def solution(mesh):
    in_specs = (
        P("row", ("depth", "col"), None, None),
        P("row", ("depth", "col")),
        P(("depth", "row"), "col", None, None),
        P(("depth", "row"), "col"),
        P(("row", "depth"), "col"),
    )
    out_specs = P(("row", "depth"), "col", None, None)
    return jax.shard_map(
        functools.partial(local, mesh), mesh=mesh, in_specs=in_specs, out_specs=out_specs, check_vma=False
    )
```

```python
import functools

import jax
import jax.numpy as jnp
import numpy as np
from jax import lax
from jax.experimental import pallas as pl
from jax.experimental.pallas import tpu as pltpu
from jax.sharding import PartitionSpec as P

LANES = 128
PARTS = 4
F32 = jnp.float32
BF16 = jnp.bfloat16
I32 = jnp.int32
SMEM = pl.BlockSpec(memory_space=pltpu.SMEM)
VMEM = pl.BlockSpec(memory_space=pltpu.VMEM)
HBM = pl.BlockSpec(memory_space=pltpu.HBM)
DMA = pltpu.SemaphoreType.DMA
PARAMS = pltpu.CompilerParams(vmem_limit_bytes=16 * 1024 * 1024)


class Plan:
    def __init__(self, mesh, a_blocks, b_blocks):
        self.nrow, self.ncol, self.ndep = (mesh.shape[name] for name in ("row", "col", "depth"))
        self.rows, self.kc, self.bs, _ = a_blocks.shape
        self.kb, self.nc, _, _ = b_blocks.shape
        assert self.kb == 1 and self.rows == self.ndep and self.nrow % 2 == 0
        every = self.nrow * self.ncol * self.ndep
        self.whole = self.bs // every >= 8
        self.axes = ("row", "col", "depth") if self.whole else ("row", "depth")
        self.G = every if self.whole else self.nrow * self.ndep
        self.stride = self.G // self.nrow
        self.R = self.bs // self.G
        self.Q = self.G * self.nc
        self.W = self.kc if self.whole else self.kc * self.ncol
        self.nk = self.kc * self.ncol * self.ndep
        self.J = 3 * self.nk // 16
        self.more = self.nk // 16
        self.slots = self.nc - 1 if self.whole else self.nc
        self.waves = 2 if self.whole else self.kc
        assert self.G & (self.G - 1) == 0 and self.nc & (self.nc - 1) == 0
        self.g_bits, self.q_bits = self.G.bit_length() - 1, self.Q.bit_length() - 1
        self.others = [(dd, dc) for dd in range(self.ndep) for dc in range(self.ncol) if (dd, dc) != (0, 0)]

    def member(self, value):
        return (value >> 2) & (self.G - 1)

    def column(self, value):
        return (value >> (2 + self.g_bits)) & (self.nc - 1)

    def slot(self, value):
        return value >> (2 + self.q_bits)

    def listed(self, rows, p, member):
        per = LANES // self.G
        return rows[p // per, p % per * self.G + member]

    def decode(self, s):
        if self.whole:
            return s // (self.ncol * self.ndep), s // self.ndep % self.ncol, s % self.ndep
        return s // self.ndep, s * 0, s % self.ndep

    def tables(self, dtype=BF16):
        q = np.arange(self.Q)[None, :]
        s = np.arange(self.G)[:, None]
        e = np.arange(LANES)[:, None]
        row_q, col_q, dep_q = self.decode(q % self.G)
        c_q = q // self.G
        row_s, col_s, dep_s = self.decode(s)
        row_t, col_t, dep_t = self.decode(s.T)
        b0 = self.rows * self.W
        select = [e == rr * self.W + row_q % self.W for rr in range(self.rows)]
        select += [e == b0 + c_q, e == b0 + self.nc + c_q, (e >= b0) & (e < b0 + c_q)]
        holds = (dep_s == dep_q) & (col_s == row_q // self.W)
        masks = [holds, s == q % self.G, col_s == col_q]
        before = np.arange(self.Q)[:, None] < q
        k = np.arange(LANES)[None, :]
        inner = (dep_q * self.nrow + row_q).T == k
        first = inner & (c_q.T == 0) & (col_q.T == 0)
        chunk = (k.T < k) & (k.T // self.kc == k // self.kc) & (k < self.nk)
        pick = [(row_s == row_t) & (dep_s == rr) for rr in range(self.rows)]
        pick += [(row_s ^ 1 == row_t) & (col_s == col_t) & (dep_s == dep_t)]
        groups = [np.concatenate(select, 1), np.concatenate(masks, 0), before, np.concatenate(pick, 1)]
        dd = (dep_s - k // self.kc // self.ncol) % self.ndep
        dc = (col_s - k // self.kc % self.ncol) % self.ncol
        away = (dd * self.ncol + dc if self.whole else np.ones_like(dd)) * (k < self.nk)
        groups += [np.concatenate([inner, first], 1), np.concatenate([chunk, away], 0)]
        return [jnp.asarray(t.astype(np.float32), dtype) for t in groups]


def dot(x, y):
    return jnp.dot(x.astype(BF16), y.astype(BF16), preferred_element_type=F32)


def dot_high(x, y):
    x_high, y_high = x.astype(BF16), y.astype(BF16)
    x_low, y_low = (x - x_high.astype(F32)).astype(BF16), (y - y_high.astype(F32)).astype(BF16)
    x_terms = jnp.concatenate([x_high, x_low, x_high], axis=1)
    return dot(x_terms, jnp.concatenate([y_low, y_high, y_high], axis=0))


def entry_row(plan, entries):
    row = entries[0:1]
    for r in range(1, plan.rows):
        row += pltpu.roll(entries[r : r + 1], r * plan.W, 1)
    return row


def entry_bits(row, start, count):
    lane = lax.broadcasted_iota(I32, row.shape, 1) - start
    return jnp.sum(jnp.where((lane >= 0) & (lane < count), row << jnp.clip(lane, 0, count - 1), 0))


def prepare(plan, entries, b_hbm, out_hbm, blocks, tile_ref, sems, out_sems):
    def piece(c, j):
        return pltpu.make_async_copy(b_hbm.at[c], blocks.at[j], sems.at[j])

    def out(src, j, width):
        return pltpu.make_async_copy(src, out_hbm.at[:, :, pl.ds(j * plan.bs, width)], out_sems.at[j])

    row = entry_row(plan, entries)
    bits = entry_bits(row, plan.rows * plan.W, plan.nc)
    count = jnp.int32(0)
    for c in range(plan.nc):
        stored = (bits >> c) & 1 == 1
        for j in range(min(c + 1, plan.slots)):

            @pl.when(stored & (count == j))
            def _(c=c, j=j):
                piece(c, j).start()

        count += stored.astype(I32)

    tile_ref[...] = jnp.broadcast_to(row.astype(F32)[None], tile_ref.shape)
    last = out(tile_ref, plan.slots, LANES)
    last.start()
    for j in range(plan.slots):

        @pl.when(count > j)
        def _(j=j):
            piece(0, j).wait()
            out(blocks.at[j], j, plan.bs).start()

    last.wait()
    for j in range(plan.slots):

        @pl.when(count > j)
        def _(j=j):
            out(blocks.at[j], j, plan.bs).wait()


def stage(plan, wave, entries, a_hbm, *refs):
    outs, sems = refs[:-1], refs[-1]
    col, dep = lax.axis_index("col"), lax.axis_index("depth")
    row = entry_row(plan, entries)
    start = 0 if plan.whole else col * plan.kc
    bits = [entry_bits(row, r * plan.W + start, plan.kc) for r in range(plan.rows)]
    stored = [[(bits[r] >> kk) & 1 == 1 for kk in range(plan.kc)] for r in range(plan.rows)]

    def each(act):
        for r in range(plan.rows):
            count = jnp.int32(0)
            for kk in range(plan.kc):
                for dd, out in enumerate(outs):

                    @pl.when(stored[r][kk] & (count == wave) & ((dep + dd) % plan.ndep == r))
                    def _(r=r, kk=kk, out=out):
                        act(pltpu.make_async_copy(a_hbm.at[r, kk], out, sems.at[r]))

                count += stored[r][kk].astype(I32)

    each(lambda copy: copy.start())
    each(lambda copy: copy.wait())


def clear(plan, _, zero_hbm, zero, sems):
    zero[...] = jnp.zeros_like(zero)
    copies = [pltpu.make_async_copy(zero, zero_hbm.at[0, c], sems.at[c]) for c in range(plan.nc)]
    for copy in copies:
        copy.start()
    for copy in copies:
        copy.wait()


def needs(plan, tile, wide, masks, before, pick):
    G, Q, rows = plan.G, plan.Q, plan.rows
    entries = dot(tile, wide[...])
    holds, own, same_col = masks[0:G], masks[G : 2 * G], masks[2 * G : 3 * G]
    stored_a = jnp.zeros((G, Q), F32)
    for rr in range(rows):
        stored_a += dot(pick[:, rr * G : (rr + 1) * G], entries[:, rr * Q : (rr + 1) * Q] * holds)
    b0 = rows * Q
    stored_b = jnp.sum(entries[:, b0 : b0 + Q] * own, axis=0, keepdims=True)
    slot = jnp.sum(entries[:, b0 + 2 * Q : b0 + 3 * Q] * own, axis=0, keepdims=True)
    need = stored_a * stored_b * entries[:, b0 + Q : b0 + 2 * Q] * same_col
    partner = dot(pick[:, rows * G :], need)
    both = jnp.maximum(need, partner)
    return need, partner, both, dot(both, before[...]), slot, stored_a


def list_blocks(plan, J, base, need, partner, both, rank, slot, out):
    G, Q, per = plan.G, plan.Q, LANES // plan.G
    q = lax.broadcasted_iota(I32, (1, Q), 1).astype(F32)
    value = 4.0 * both * (slot * float(Q) + q) + 2.0 * partner + need
    member = lax.broadcasted_iota(I32, (G, LANES), 0)
    lane = lax.broadcasted_iota(I32, (G, LANES), 1)
    turn = rank - ((member[:, :1] >> (plan.stride.bit_length() - 1)) & 1).astype(F32) - base
    for n in range(out.shape[0]):
        row = jnp.zeros((G, LANES), F32)
        for p in range(n * per, min((n + 1) * per, J)):
            at = jnp.sum(jnp.where(turn == 2.0 * p, value, 0.0), axis=1, keepdims=True)
            row = jnp.where(lane == p % per * G + member, at, row)
        out[n : n + 1] = jnp.sum(row, axis=0, keepdims=True).astype(I32)


def schedule(plan, J, base, tile_ref, got_ref, *refs):
    tables, rest, refs = refs[:4], refs[4:-7], refs[-7:]
    out_hbm, rows_ref, facts_ref, pieces, scratch, sem, out_sems = refs
    start = 0.0 if base is None else base[0].astype(F32)
    need, partner, both, rank, slot, stored_a = needs(plan, tile_ref[:, 0, tile_ref.shape[2] - LANES :], *tables)
    list_blocks(plan, J, start, need, partner, both, rank, slot, rows_ref)
    copy = pltpu.make_async_copy(rows_ref, scratch, sem.at[0])
    copy.start()
    for n, fact in enumerate((need, both, stored_a, jnp.broadcast_to(slot, need.shape))):
        facts_ref[n] = fact
    copy.wait()

    def take(d):
        for p in range(J):
            value = plan.listed(scratch, p, d)
            slot = plan.slot(value)
            lane = pl.multiple_of(jnp.minimum(slot, plan.slots - 1) * plan.bs, plan.bs)
            pieces[d, p] = got_ref[plan.member(value), :, pl.ds(lane, plan.bs)]
            if rest:

                @pl.when(slot >= plan.slots)
                def _():
                    pieces[d, p] = rest[0][plan.member(value)]

    size = plan.G // PARTS
    copies = []
    for n in range(PARTS):
        part = pl.ds(n * size, size)
        copies.append(pltpu.make_async_copy(pieces.at[part], out_hbm.at[part], out_sems.at[n]))

        @pl.loop(n * size, (n + 1) * size, unroll=1 if rest else size)
        def _(d):
            take(d)

        copies[n].start()
    for copy in copies:
        copy.wait()


def settle(plan, wave, facts_ref, inner, chunk, a_hbm, *refs):
    outs, (all_ref, place_ref, place_smem, sems) = refs[:-4], refs[-4:]
    need, stored_a = facts_ref[0], facts_ref[2]
    before = chunk[0:LANES]
    left = jnp.minimum(dot(need, inner[:, :LANES]), 1.0)
    place = dot(dot(stored_a, inner[:, LANES:]), before)
    if plan.whole:
        late = jnp.where(place > 0, left, 0.0)
        place = jnp.where(place > 0, jnp.where(late > 0, 1.0 + dot(late, before), -1.0), 0.0)
    all_ref[...] = place
    row, col, dep = lax.axis_index("row"), lax.axis_index("col"), lax.axis_index("depth")
    member = lax.broadcasted_iota(I32, place.shape, 0)
    owners = []
    for dd, dc in plan.others[: len(outs)]:
        to_dep, to_col = (dep + dd) % plan.ndep, (col + dc) % plan.ncol
        owners.append((to_dep, (row * plan.ncol + to_col) * plan.ndep + to_dep))
    for o, (_, to) in enumerate(owners):
        place_ref[o : o + 1] = jnp.sum(jnp.where(member == to, place, 0.0), axis=0, keepdims=True).astype(I32)
    fetch = pltpu.make_async_copy(place_ref, place_smem, sems.at[len(outs)])
    fetch.start()

    def each(act):
        for o, out in enumerate(outs):
            to_dep = owners[o][0]
            for kk in range(plan.kc):

                @pl.when(place_smem[o, dep * plan.nrow + col * plan.kc + kk] == wave)
                def _(o=o, kk=kk, out=out, to_dep=to_dep):
                    act(pltpu.make_async_copy(a_hbm.at[to_dep, kk], out, sems.at[o]))

    fetch.wait()
    each(lambda copy: copy.start())
    each(lambda copy: copy.wait())


def judge(plan, facts_ref, place_ref, rows_ref, inner, chunk, _, waves_ref, waves_again, rows_again, state_ref):
    rows_again[...] = rows_ref[...]
    need, both, slot, place = facts_ref[0], facts_ref[1], facts_ref[3], place_ref[...]
    away = chunk[LANES:].astype(F32)
    left = jnp.minimum(dot(need, inner[:, :LANES]), 1.0)
    member = lax.broadcasted_iota(I32, place.shape, 0)
    mine = jnp.where(member == lax.axis_index(plan.axes), place, 0.0)
    waves_ref[...] = jnp.sum(mine, axis=0, keepdims=True).astype(I32)
    waves_again[...] = waves_ref[...]
    most = jnp.max(jnp.sum(both, axis=1, keepdims=True)).astype(I32)
    lost = jnp.max(need * jnp.where(slot >= plan.slots, 1.0, 0.0)) > 0
    waves = jnp.max(left * jnp.where(away > 0, 1.0, 0.0) * (place + 1.0))
    last = left * jnp.where(place == float(plan.waves), 1.0, 0.0) * away
    count = len(plan.others) if plan.whole else 0
    way = jnp.int32(2 + count)
    for o in range(count):
        way = jnp.where(jnp.max(jnp.where(last == o + 1.0, 0.0, last)) == 0.0, 2 + o, way)
    easy = jnp.where(lost, 3 + count, jnp.where(most > 2 * plan.J, 1, 0))
    hard = jnp.where((waves > plan.waves + 1) | lost, 4 + count, way)
    state_ref[0] = jnp.where(waves > plan.waves, hard, easy)
    state_ref[1] = most


def multiply(plan, J, raw, waves, first, rows, left, mine, theirs, a_hbm, *refs):
    lefts, refs = refs[: waves * len(plan.others)], refs[waves * len(plan.others) :]
    _, out_hbm, a_scr, total, sems, out_sems = refs
    col, dep = lax.axis_index("col"), lax.axis_index("depth")
    member = lax.axis_index(plan.axes)
    listed = [plan.listed(rows, p, member) for p in range(J)]
    listed += [plan.listed(rows, p, member ^ plan.stride) >> 1 << 1 for p in range(J)]
    asked = [value & 1 for value in listed[: J]] + [(value >> 1) & 1 for value in listed[J :]]

    def copy(src, j):
        return pltpu.make_async_copy(src, a_scr.at[j], sems.at[j])

    ready = []
    for j, value in enumerate(listed):
        row_s, _, dep_s = plan.decode(plan.member(value))
        dd = (dep - dep_s + plan.ndep) % plan.ndep
        dc = (col - row_s // plan.kc + plan.ncol) % plan.ncol
        kk = row_s % plan.kc
        near = (dd == 0) & (dc == 0)
        wave = jnp.int32(0) if raw else left[0, dep_s * plan.nrow + row_s]
        ready.append((asked[j] == 1) & (near | (wave < waves)))

        @pl.when(ready[j])
        def _(j=j, kk=kk, dd=dd, dc=dc, near=near, wave=wave):
            @pl.when(near)
            def _():
                copy(a_hbm.at[dep, kk], j).start()

            for n, (xd, xc) in enumerate(plan.others):
                for w in range(waves):

                    @pl.when((dd == xd) & (dc == xc) & (wave == w))
                    def _(n=n, w=w):
                        src = lefts[w * len(plan.others) + n]
                        copy(src.at[kk] if raw else src, j).start()

    def block(c):
        return pltpu.make_async_copy(total.at[c], out_hbm.at[0, c], out_sems.at[c])

    column = [plan.column(value) for value in listed]
    touched = [functools.reduce(jnp.logical_or, [r & (x == c) for r, x in zip(ready, column)]) for c in range(plan.nc)]
    for c in range(plan.nc):

        @pl.when(touched[c])
        def _(c=c):
            if first:
                total[c] = jnp.zeros((plan.bs, plan.bs), F32)
            else:
                begin = pltpu.make_async_copy(out_hbm.at[0, c], total.at[c], out_sems.at[c])
                begin.start()
                begin.wait()

    for j in range(2 * J):

        @pl.when(ready[j])
        def _(j=j):
            source = mine if j < J else theirs
            right = source[:, j % J].reshape(plan.bs, plan.bs)
            copy(a_hbm.at[0, 0], j).wait()
            total[column[j]] += dot_high(a_scr[j], right)

    for act in (lambda copy: copy.start(), lambda copy: copy.wait()):
        for c in range(plan.nc):
            pl.when(touched[c])(lambda c=c, act=act: act(block(c)))


def call(kernel, out_shape, in_specs, out_specs, scratch=(), **kwargs):
    return pl.pallas_call(
        kernel,
        out_shape=out_shape,
        in_specs=in_specs,
        out_specs=out_specs,
        scratch_shapes=scratch,
        compiler_params=PARAMS,
        name=kernel.func.__name__,
        **kwargs,
    )


def local(mesh, a_blocks, a_pattern, b_blocks, b_pattern, c_pattern):
    plan = Plan(mesh, a_blocks, b_blocks)
    G, R, J, bs, nc = plan.G, plan.R, plan.J, plan.bs, plan.nc
    result = jax.ShapeDtypeStruct((1, nc, bs, bs), F32)
    block = jax.ShapeDtypeStruct((bs, bs), F32)

    def exchange(pieces):
        return lax.all_to_all(pieces, plan.axes, 0, 0, tiled=True)

    def shift(staged, only=None):
        def perm(dd, dc):
            for x in range(plan.ncol):
                for y in range(plan.ndep):
                    yield x * plan.ndep + y, (x + dc) % plan.ncol * plan.ndep + (y + dd) % plan.ndep

        names = range(len(staged)) if only is None else only
        return [lax.ppermute(staged[o], ("col", "depth"), list(perm(*plan.others[o]))) for o in names]

    def swap(mine):
        return lax.ppermute(mine, "row", [(i, i ^ 1) for i in range(plan.nrow)])

    def listed(J, base, got, rest, tables):
        first = base is None
        listing = (-(-J * G // LANES), LANES)
        return call(
            functools.partial(schedule, plan, J, *(None,) * first),
            (
                jax.ShapeDtypeStruct((G, J, R, bs), F32),
                jax.ShapeDtypeStruct(listing, I32),
                jax.ShapeDtypeStruct((4, G, plan.Q), F32),
            ),
            [SMEM] * (not first) + [VMEM] * (6 + len(rest)),
            (HBM, VMEM, VMEM),
            [pltpu.VMEM((G, J, R, bs), F32), pltpu.SMEM(listing, I32), DMA((1,)), DMA((PARTS,))],
        )(*[] if first else [jnp.reshape(base, (1,))], got, got, *tables[:4], *rest)

    def settled(wave, facts, a_blocks, tables):
        count = len(plan.others) if plan.whole else 0
        *sent, place = call(
            functools.partial(settle, plan, wave),
            (block,) * count + (jax.ShapeDtypeStruct((G, LANES), F32),),
            [VMEM] * 3 + [HBM],
            (VMEM,) * (count + 1),
            [pltpu.VMEM((8, LANES), I32), pltpu.SMEM((8, LANES), I32), DMA((count + 1,))],
        )(facts, *tables[4:], a_blocks)
        return sent, place

    def judged(facts, place, rows, tables, after):
        line = jax.ShapeDtypeStruct((1, LANES), I32)
        shapes = (line, line, jax.ShapeDtypeStruct(rows.shape, I32), jax.ShapeDtypeStruct((2,), I32))
        kernel = functools.partial(judge, plan)
        return call(kernel, shapes, [VMEM] * 6, (VMEM, VMEM, VMEM, SMEM))(facts, place, rows, *tables[4:], after)

    def product(J, raw, first, rows, waves, mine, theirs, a_blocks, lefts, start):
        return call(
            functools.partial(multiply, plan, J, raw, len(lefts) // len(plan.others), first),
            result,
            [SMEM, SMEM, VMEM, VMEM] + [HBM] * (2 + len(lefts)),
            HBM,
            [
                pltpu.VMEM((2 * J, bs, bs), F32),
                pltpu.VMEM((nc, bs, bs), F32),
                DMA((2 * J,)),
                DMA((nc,)),
            ],
            input_output_aliases={5 + len(lefts): 0},
        )(rows, waves, mine, theirs, a_blocks, *lefts, start)

    if not plan.whole:
        a_pattern = lax.all_gather(a_pattern, "col", axis=1, tiled=True)
    b0 = plan.rows * plan.W
    entries = jnp.pad(b_pattern, ((0, plan.rows - 1), (b0, LANES - b0 - nc)))
    entries += jnp.pad(c_pattern, ((0, plan.rows - 1), (b0 + nc, LANES - b0 - 2 * nc)))
    entries += jnp.pad(a_pattern, ((0, 0), (0, LANES - plan.W)))

    b_pieces = b_blocks.reshape(nc, G, R, bs)
    width = plan.slots * bs + LANES
    pieces = call(
        functools.partial(prepare, plan),
        jax.ShapeDtypeStruct((G, R, width), F32),
        [VMEM, HBM],
        HBM,
        [
            pltpu.VMEM((plan.slots, G, R, bs), F32),
            pltpu.VMEM((G, R, LANES), F32),
            DMA((plan.slots,)),
            DMA((plan.slots + 1,)),
        ],
    )(entries, b_pieces)
    got = exchange(pieces)
    lefts = []
    for wave in range(1 if plan.whole else plan.waves):
        staged = call(
            functools.partial(stage, plan, wave),
            (block,) * plan.ndep,
            [VMEM, HBM],
            (VMEM,) * plan.ndep,
            [DMA((plan.rows,))],
        )(entries, a_blocks)
        lefts += shift([staged[dd] for dd, _ in plan.others])

    tables = plan.tables()
    zero = call(
        functools.partial(clear, plan), result, [VMEM], HBM, [pltpu.VMEM((bs, bs), F32), DMA((nc,))]
    )(staged[0])
    got, lefts, zero = lax.optimization_barrier((got, lefts, zero))
    send, rows, facts = listed(J, None, got, [], tables)
    mine = exchange(send)
    sent, place = settled(1, facts, a_blocks, tables)
    waves, waves_again, rows_again, state = judged(facts, place, rows, tables, sent[0] if sent else place)
    sent = shift(sent)
    mine, sent = lax.optimization_barrier((mine, sent))
    lefts = lefts + sent
    theirs = swap(mine)
    near = [pltpu.with_memory_space_constraint(x, pltpu.VMEM) for x in (mine, theirs)]
    c_blocks = product(J, False, True, rows, waves, *near, a_blocks, lefts, zero)

    again = plan.tables(F32)

    def rounds(J, begin, raw, rest, got, state, waves, a_blocks, lefts, c_blocks):
        most = state[1] if plan.whole else lax.pmax(state[1], "col")

        def body(turn, c_blocks):
            send, rows, _ = listed(J, begin + 2 * J * turn, got, rest, again)
            mine = exchange(send)
            return product(J, raw, False, rows, waves, mine, swap(mine), a_blocks, lefts, c_blocks)

        return lax.fori_loop(0, (jnp.maximum(most - begin, 0) + 2 * J - 1) // (2 * J), body, c_blocks)

    def spread_rest(b_pieces):
        return [exchange(b_pieces[plan.slots])] if plan.slots < nc else []

    def done(c_blocks, *_):
        return c_blocks

    def more_rounds(c_blocks, rows, mine, theirs, got, facts, state, waves, a_blocks, b_pieces, *lefts):
        return rounds(plan.more, 2 * J, False, [], got, state, waves, a_blocks, lefts, c_blocks)

    def more_waves(way, c_blocks, rows, mine, theirs, got, facts, state, waves, a_blocks, b_pieces, *lefts):
        sent = settled(2, facts, a_blocks, again)[0]
        for o in range(len(sent)):
            if way in (o, len(sent)):
                sent[o] = shift(sent, [o])[0]
        c_blocks = product(J, False, True, rows, waves, mine, theirs, a_blocks, lefts + tuple(sent), c_blocks)
        return rounds(plan.more, 2 * J, False, [], got, state, waves, a_blocks, lefts + tuple(sent), c_blocks)

    def more_pieces(c_blocks, rows, mine, theirs, got, facts, state, waves, a_blocks, b_pieces, *lefts):
        c_blocks = jnp.zeros_like(c_blocks)
        return rounds(J, 0, False, spread_rest(b_pieces), got, state, waves, a_blocks, lefts, c_blocks)

    def anew(c_blocks, rows, mine, theirs, got, facts, state, waves, a_blocks, b_pieces, *lefts):
        c_blocks = jnp.zeros_like(c_blocks)
        dep = lax.axis_index("depth")
        raw = [lax.dynamic_index_in_dim(a_blocks, (dep + dd) % plan.ndep, keepdims=False) for dd, _ in plan.others]
        return rounds(J, 0, True, spread_rest(b_pieces), got, state, waves, a_blocks, shift(raw), c_blocks)

    index = state[0] if plan.whole else lax.pmax(state[0], "col")
    ways = [functools.partial(more_waves, way) for way in range(len(plan.others) * plan.whole + 1)]
    branches = [done, more_rounds, *ways, more_pieces, anew]
    kept = (rows_again, mine, theirs, got, facts, state, waves_again, a_blocks, b_pieces)
    return lax.switch(index, branches, c_blocks, *kept, *lefts)


def solution(mesh):
    in_specs = (
        P("row", ("depth", "col"), None, None),
        P("row", ("depth", "col")),
        P(("depth", "row"), "col", None, None),
        P(("depth", "row"), "col"),
        P(("row", "depth"), "col"),
    )
    out_specs = P(("row", "depth"), "col", None, None)
    return jax.shard_map(
        functools.partial(local, mesh), mesh=mesh, in_specs=in_specs, out_specs=out_specs, check_vma=False
    )
```

```python
import functools

import jax
import jax.numpy as jnp
import numpy as np
from jax import lax
from jax.experimental import pallas as pl
from jax.experimental.pallas import tpu as pltpu
from jax.sharding import PartitionSpec as P

LANES = 128
PARTS = 4
F32 = jnp.float32
BF16 = jnp.bfloat16
I32 = jnp.int32
SMEM = pl.BlockSpec(memory_space=pltpu.SMEM)
VMEM = pl.BlockSpec(memory_space=pltpu.VMEM)
HBM = pl.BlockSpec(memory_space=pltpu.HBM)
DMA = pltpu.SemaphoreType.DMA
PARAMS = pltpu.CompilerParams(vmem_limit_bytes=16 * 1024 * 1024)


class Plan:
    def __init__(self, mesh, a_blocks, b_blocks):
        self.nrow, self.ncol, self.ndep = (mesh.shape[name] for name in ("row", "col", "depth"))
        self.rows, self.kc, self.bs, _ = a_blocks.shape
        self.kb, self.nc, _, _ = b_blocks.shape
        assert self.kb == 1 and self.rows == self.ndep and self.nrow % 2 == 0
        every = self.nrow * self.ncol * self.ndep
        self.whole = self.bs // every >= 8
        self.axes = ("row", "col", "depth") if self.whole else ("row", "depth")
        self.G = every if self.whole else self.nrow * self.ndep
        self.stride = self.G // self.nrow
        self.R = self.bs // self.G
        self.Q = self.G * self.nc
        self.W = self.kc if self.whole else self.kc * self.ncol
        self.nk = self.kc * self.ncol * self.ndep
        self.J = 3 * self.nk // 16
        self.more = self.nk // 16
        self.slots = self.nc - 1 if self.whole else self.nc
        self.waves = 2 if self.whole else self.kc
        assert self.G & (self.G - 1) == 0 and self.nc & (self.nc - 1) == 0
        self.g_bits, self.q_bits = self.G.bit_length() - 1, self.Q.bit_length() - 1
        self.others = [(dd, dc) for dd in range(self.ndep) for dc in range(self.ncol) if (dd, dc) != (0, 0)]

    def member(self, value):
        return (value >> 2) & (self.G - 1)

    def column(self, value):
        return (value >> (2 + self.g_bits)) & (self.nc - 1)

    def slot(self, value):
        return value >> (2 + self.q_bits)

    def listed(self, rows, p, member):
        per = LANES // self.G
        return rows[p // per, p % per * self.G + member]

    def decode(self, s):
        if self.whole:
            return s // (self.ncol * self.ndep), s // self.ndep % self.ncol, s % self.ndep
        return s // self.ndep, s * 0, s % self.ndep

    def tables(self, dtype=BF16):
        q = np.arange(self.Q)[None, :]
        s = np.arange(self.G)[:, None]
        e = np.arange(LANES)[:, None]
        row_q, col_q, dep_q = self.decode(q % self.G)
        c_q = q // self.G
        row_s, col_s, dep_s = self.decode(s)
        row_t, col_t, dep_t = self.decode(s.T)
        b0 = self.rows * self.W
        select = [e == rr * self.W + row_q % self.W for rr in range(self.rows)]
        select += [e == b0 + c_q, e == b0 + self.nc + c_q, (e >= b0) & (e < b0 + c_q)]
        holds = (dep_s == dep_q) & (col_s == row_q // self.W)
        masks = [holds, s == q % self.G, col_s == col_q]
        before = np.arange(self.Q)[:, None] < q
        k = np.arange(LANES)[None, :]
        inner = (dep_q * self.nrow + row_q).T == k
        first = inner & (c_q.T == 0) & (col_q.T == 0)
        chunk = (k.T < k) & (k.T // self.kc == k // self.kc) & (k < self.nk)
        pick = [(row_s == row_t) & (dep_s == rr) for rr in range(self.rows)]
        pick += [(row_s ^ 1 == row_t) & (col_s == col_t) & (dep_s == dep_t)]
        groups = [np.concatenate(select, 1), np.concatenate(masks, 0), before, np.concatenate(pick, 1)]
        dd = (dep_s - k // self.kc // self.ncol) % self.ndep
        dc = (col_s - k // self.kc % self.ncol) % self.ncol
        away = (dd * self.ncol + dc if self.whole else np.ones_like(dd)) * (k < self.nk)
        groups += [np.concatenate([inner, first], 1), np.concatenate([chunk, away], 0)]
        return [jnp.asarray(t.astype(np.float32), dtype) for t in groups]


def dot(x, y):
    return jnp.dot(x.astype(BF16), y.astype(BF16), preferred_element_type=F32)


def dot_high(x, y):
    x_high, y_high = x.astype(BF16), y.astype(BF16)
    x_low, y_low = (x - x_high.astype(F32)).astype(BF16), (y - y_high.astype(F32)).astype(BF16)
    x_terms = jnp.concatenate([x_high, x_low, x_high], axis=1)
    return dot(x_terms, jnp.concatenate([y_low, y_high, y_high], axis=0))


def entry_row(plan, entries):
    row = entries[0:1]
    for r in range(1, plan.rows):
        row += pltpu.roll(entries[r : r + 1], r * plan.W, 1)
    return row


def entry_bits(row, start, count):
    lane = lax.broadcasted_iota(I32, row.shape, 1) - start
    return jnp.sum(jnp.where((lane >= 0) & (lane < count), row << jnp.clip(lane, 0, count - 1), 0))


def prepare(plan, entries, b_hbm, out_hbm, blocks, tile_ref, sems, out_sems):
    half = plan.G // 2

    def piece(c, j, n):
        part = pl.ds(n * half, half)
        return pltpu.make_async_copy(b_hbm.at[c, part], blocks.at[j, part], sems.at[j, n])

    def out(j, n):
        part = pl.ds(n * half, half)
        dst = out_hbm.at[part, :, pl.ds(j * plan.bs, plan.bs)]
        return pltpu.make_async_copy(blocks.at[j, part], dst, out_sems.at[j, n])

    row = entry_row(plan, entries)
    bits = entry_bits(row, plan.rows * plan.W, plan.nc)
    count = jnp.int32(0)
    for c in range(plan.nc):
        stored = (bits >> c) & 1 == 1
        for j in range(min(c + 1, plan.slots)):

            @pl.when(stored & (count == j))
            def _(c=c, j=j):
                piece(c, j, 0).start()
                piece(c, j, 1).start()

        count += stored.astype(I32)

    tile_ref[...] = jnp.broadcast_to(row.astype(F32)[None], tile_ref.shape)
    lanes = pl.ds(plan.slots * plan.bs, LANES)
    last = pltpu.make_async_copy(tile_ref, out_hbm.at[:, :, lanes], out_sems.at[plan.slots, 0])
    last.start()
    for j in range(plan.slots):

        @pl.when(count > j)
        def _(j=j):
            for n in range(2):
                piece(0, j, n).wait()
                out(j, n).start()

    last.wait()
    for j in range(plan.slots):

        @pl.when(count > j)
        def _(j=j):
            for n in range(2):
                out(j, n).wait()


def stage(plan, wave, entries, a_hbm, *refs):
    outs, sems = refs[:-1], refs[-1]
    col, dep = lax.axis_index("col"), lax.axis_index("depth")
    row = entry_row(plan, entries)
    start = 0 if plan.whole else col * plan.kc
    bits = [entry_bits(row, r * plan.W + start, plan.kc) for r in range(plan.rows)]
    stored = [[(bits[r] >> kk) & 1 == 1 for kk in range(plan.kc)] for r in range(plan.rows)]

    def each(act):
        for r in range(plan.rows):
            count = jnp.int32(0)
            for kk in range(plan.kc):
                for dd, out in enumerate(outs):

                    @pl.when(stored[r][kk] & (count == wave) & ((dep + dd) % plan.ndep == r))
                    def _(r=r, kk=kk, out=out):
                        act(pltpu.make_async_copy(a_hbm.at[r, kk], out, sems.at[r]))

                count += stored[r][kk].astype(I32)

    each(lambda copy: copy.start())
    each(lambda copy: copy.wait())


def clear(plan, _, zero_hbm, zero, sems):
    zero[...] = jnp.zeros_like(zero)
    copies = [pltpu.make_async_copy(zero, zero_hbm.at[0, c], sems.at[c]) for c in range(plan.nc)]
    for copy in copies:
        copy.start()
    for copy in copies:
        copy.wait()


def needs(plan, tile, wide, masks, before, pick):
    G, Q, rows = plan.G, plan.Q, plan.rows
    entries = dot(tile, wide[...])
    holds, own, same_col = masks[0:G], masks[G : 2 * G], masks[2 * G : 3 * G]
    stored_a = jnp.zeros((G, Q), F32)
    for rr in range(rows):
        stored_a += dot(pick[:, rr * G : (rr + 1) * G], entries[:, rr * Q : (rr + 1) * Q] * holds)
    b0 = rows * Q
    stored_b = jnp.sum(entries[:, b0 : b0 + Q] * own, axis=0, keepdims=True)
    slot = jnp.sum(entries[:, b0 + 2 * Q : b0 + 3 * Q] * own, axis=0, keepdims=True)
    need = stored_a * stored_b * entries[:, b0 + Q : b0 + 2 * Q] * same_col
    partner = dot(pick[:, rows * G :], need)
    both = jnp.maximum(need, partner)
    return need, partner, both, dot(both, before[...]), slot, stored_a


def list_blocks(plan, J, base, need, partner, both, rank, slot, out):
    G, Q, per = plan.G, plan.Q, LANES // plan.G
    q = lax.broadcasted_iota(I32, (1, Q), 1).astype(F32)
    value = 4.0 * both * (slot * float(Q) + q) + 2.0 * partner + need
    member = lax.broadcasted_iota(I32, (G, LANES), 0)
    lane = lax.broadcasted_iota(I32, (G, LANES), 1)
    turn = rank - ((member[:, :1] >> (plan.stride.bit_length() - 1)) & 1).astype(F32) - base
    for n in range(out.shape[0]):
        row = jnp.zeros((G, LANES), F32)
        for p in range(n * per, min((n + 1) * per, J)):
            at = jnp.sum(jnp.where(turn == 2.0 * p, value, 0.0), axis=1, keepdims=True)
            row = jnp.where(lane == p % per * G + member, at, row)
        out[n : n + 1] = jnp.sum(row, axis=0, keepdims=True).astype(I32)


def schedule(plan, J, base, tile_ref, got_ref, *refs):
    tables, rest, refs = refs[:4], refs[4:-7], refs[-7:]
    out_hbm, rows_ref, facts_ref, pieces, scratch, sem, out_sems = refs
    start = 0.0 if base is None else base[0].astype(F32)
    need, partner, both, rank, slot, stored_a = needs(plan, tile_ref[:, 0, tile_ref.shape[2] - LANES :], *tables)
    list_blocks(plan, J, start, need, partner, both, rank, slot, rows_ref)
    copy = pltpu.make_async_copy(rows_ref, scratch, sem.at[0])
    copy.start()
    for n, fact in enumerate((need, both, stored_a, jnp.broadcast_to(slot, need.shape))):
        facts_ref[n] = fact
    copy.wait()

    def take(d):
        for p in range(J):
            value = plan.listed(scratch, p, d)
            slot = plan.slot(value)
            lane = pl.multiple_of(jnp.minimum(slot, plan.slots - 1) * plan.bs, plan.bs)
            pieces[d, p] = got_ref[plan.member(value), :, pl.ds(lane, plan.bs)]
            if rest:

                @pl.when(slot >= plan.slots)
                def _():
                    pieces[d, p] = rest[0][plan.member(value)]

    size = plan.G // PARTS
    copies = []
    for n in range(PARTS):
        part = pl.ds(n * size, size)
        copies.append(pltpu.make_async_copy(pieces.at[part], out_hbm.at[part], out_sems.at[n]))

        @pl.loop(n * size, (n + 1) * size, unroll=1 if rest else size)
        def _(d):
            take(d)

        copies[n].start()
    for copy in copies:
        copy.wait()


def settle(plan, wave, facts_ref, inner, chunk, a_hbm, *refs):
    outs, (all_ref, place_ref, place_smem, sems) = refs[:-4], refs[-4:]
    need, stored_a = facts_ref[0], facts_ref[2]
    before = chunk[0:LANES]
    left = jnp.minimum(dot(need, inner[:, :LANES]), 1.0)
    place = dot(dot(stored_a, inner[:, LANES:]), before)
    if plan.whole:
        late = jnp.where(place > 0, left, 0.0)
        place = jnp.where(place > 0, jnp.where(late > 0, 1.0 + dot(late, before), -1.0), 0.0)
    all_ref[...] = place
    row, col, dep = lax.axis_index("row"), lax.axis_index("col"), lax.axis_index("depth")
    member = lax.broadcasted_iota(I32, place.shape, 0)
    owners = []
    for dd, dc in plan.others[: len(outs)]:
        to_dep, to_col = (dep + dd) % plan.ndep, (col + dc) % plan.ncol
        owners.append((to_dep, (row * plan.ncol + to_col) * plan.ndep + to_dep))
    for o, (_, to) in enumerate(owners):
        place_ref[o : o + 1] = jnp.sum(jnp.where(member == to, place, 0.0), axis=0, keepdims=True).astype(I32)
    fetch = pltpu.make_async_copy(place_ref, place_smem, sems.at[len(outs)])
    fetch.start()

    def each(act):
        for o, out in enumerate(outs):
            to_dep = owners[o][0]
            for kk in range(plan.kc):

                @pl.when(place_smem[o, dep * plan.nrow + col * plan.kc + kk] == wave)
                def _(o=o, kk=kk, out=out, to_dep=to_dep):
                    act(pltpu.make_async_copy(a_hbm.at[to_dep, kk], out, sems.at[o]))

    fetch.wait()
    each(lambda copy: copy.start())
    each(lambda copy: copy.wait())


def judge(plan, facts_ref, place_ref, rows_ref, inner, chunk, _, waves_ref, waves_again, rows_again, state_ref):
    rows_again[...] = rows_ref[...]
    need, both, slot, place = facts_ref[0], facts_ref[1], facts_ref[3], place_ref[...]
    away = chunk[LANES:].astype(F32)
    left = jnp.minimum(dot(need, inner[:, :LANES]), 1.0)
    member = lax.broadcasted_iota(I32, place.shape, 0)
    mine = jnp.where(member == lax.axis_index(plan.axes), place, 0.0)
    waves_ref[...] = jnp.sum(mine, axis=0, keepdims=True).astype(I32)
    waves_again[...] = waves_ref[...]
    most = jnp.max(jnp.sum(both, axis=1, keepdims=True)).astype(I32)
    lost = jnp.max(need * jnp.where(slot >= plan.slots, 1.0, 0.0)) > 0
    waves = jnp.max(left * jnp.where(away > 0, 1.0, 0.0) * (place + 1.0))
    last = left * jnp.where(place == float(plan.waves), 1.0, 0.0) * away
    count = len(plan.others) if plan.whole else 0
    way = jnp.int32(2 + count)
    for o in range(count):
        way = jnp.where(jnp.max(jnp.where(last == o + 1.0, 0.0, last)) == 0.0, 2 + o, way)
    easy = jnp.where(lost, 3 + count, jnp.where(most > 2 * plan.J, 1, 0))
    hard = jnp.where((waves > plan.waves + 1) | lost, 4 + count, way)
    state_ref[0] = jnp.where(waves > plan.waves, hard, easy)
    state_ref[1] = most


def multiply(plan, J, raw, waves, first, rows, left, mine, theirs, a_hbm, *refs):
    lefts, refs = refs[: waves * len(plan.others)], refs[waves * len(plan.others) :]
    _, out_hbm, a_scr, total, sems, out_sems = refs
    col, dep = lax.axis_index("col"), lax.axis_index("depth")
    member = lax.axis_index(plan.axes)
    listed = [plan.listed(rows, p, member) for p in range(J)]
    listed += [plan.listed(rows, p, member ^ plan.stride) >> 1 << 1 for p in range(J)]
    asked = [value & 1 for value in listed[: J]] + [(value >> 1) & 1 for value in listed[J :]]

    def copy(src, j):
        return pltpu.make_async_copy(src, a_scr.at[j], sems.at[j])

    ready = []
    for j, value in enumerate(listed):
        row_s, _, dep_s = plan.decode(plan.member(value))
        dd = (dep - dep_s + plan.ndep) % plan.ndep
        dc = (col - row_s // plan.kc + plan.ncol) % plan.ncol
        kk = row_s % plan.kc
        near = (dd == 0) & (dc == 0)
        wave = jnp.int32(0) if raw else left[0, dep_s * plan.nrow + row_s]
        ready.append((asked[j] == 1) & (near | (wave < waves)))

        @pl.when(ready[j])
        def _(j=j, kk=kk, dd=dd, dc=dc, near=near, wave=wave):
            @pl.when(near)
            def _():
                copy(a_hbm.at[dep, kk], j).start()

            for n, (xd, xc) in enumerate(plan.others):
                for w in range(waves):

                    @pl.when((dd == xd) & (dc == xc) & (wave == w))
                    def _(n=n, w=w):
                        src = lefts[w * len(plan.others) + n]
                        copy(src.at[kk] if raw else src, j).start()

    def block(c):
        return pltpu.make_async_copy(total.at[c], out_hbm.at[0, c], out_sems.at[c])

    column = [plan.column(value) for value in listed]
    touched = [functools.reduce(jnp.logical_or, [r & (x == c) for r, x in zip(ready, column)]) for c in range(plan.nc)]
    for c in range(plan.nc):

        @pl.when(touched[c])
        def _(c=c):
            if first:
                total[c] = jnp.zeros((plan.bs, plan.bs), F32)
            else:
                begin = pltpu.make_async_copy(out_hbm.at[0, c], total.at[c], out_sems.at[c])
                begin.start()
                begin.wait()

    for j in range(2 * J):

        @pl.when(ready[j])
        def _(j=j):
            source = mine if j < J else theirs
            right = source[:, j % J].reshape(plan.bs, plan.bs)
            copy(a_hbm.at[0, 0], j).wait()
            total[column[j]] += dot_high(a_scr[j], right)

    for act in (lambda copy: copy.start(), lambda copy: copy.wait()):
        for c in range(plan.nc):
            pl.when(touched[c])(lambda c=c, act=act: act(block(c)))


def call(kernel, out_shape, in_specs, out_specs, scratch=(), **kwargs):
    return pl.pallas_call(
        kernel,
        out_shape=out_shape,
        in_specs=in_specs,
        out_specs=out_specs,
        scratch_shapes=scratch,
        compiler_params=PARAMS,
        name=kernel.func.__name__,
        **kwargs,
    )


def local(mesh, a_blocks, a_pattern, b_blocks, b_pattern, c_pattern):
    plan = Plan(mesh, a_blocks, b_blocks)
    G, R, J, bs, nc = plan.G, plan.R, plan.J, plan.bs, plan.nc
    result = jax.ShapeDtypeStruct((1, nc, bs, bs), F32)
    block = jax.ShapeDtypeStruct((bs, bs), F32)

    def exchange(pieces):
        return lax.all_to_all(pieces, plan.axes, 0, 0, tiled=True)

    def shift(staged, only=None):
        def perm(dd, dc):
            for x in range(plan.ncol):
                for y in range(plan.ndep):
                    yield x * plan.ndep + y, (x + dc) % plan.ncol * plan.ndep + (y + dd) % plan.ndep

        names = range(len(staged)) if only is None else only
        return [lax.ppermute(staged[o], ("col", "depth"), list(perm(*plan.others[o]))) for o in names]

    def swap(mine):
        return lax.ppermute(mine, "row", [(i, i ^ 1) for i in range(plan.nrow)])

    def listed(J, base, got, rest, tables):
        first = base is None
        listing = (-(-J * G // LANES), LANES)
        return call(
            functools.partial(schedule, plan, J, *(None,) * first),
            (
                jax.ShapeDtypeStruct((G, J, R, bs), F32),
                jax.ShapeDtypeStruct(listing, I32),
                jax.ShapeDtypeStruct((4, G, plan.Q), F32),
            ),
            [SMEM] * (not first) + [VMEM] * (6 + len(rest)),
            (HBM, VMEM, VMEM),
            [pltpu.VMEM((G, J, R, bs), F32), pltpu.SMEM(listing, I32), DMA((1,)), DMA((PARTS,))],
        )(*[] if first else [jnp.reshape(base, (1,))], got, got, *tables[:4], *rest)

    def settled(wave, facts, a_blocks, tables):
        count = len(plan.others) if plan.whole else 0
        *sent, place = call(
            functools.partial(settle, plan, wave),
            (block,) * count + (jax.ShapeDtypeStruct((G, LANES), F32),),
            [VMEM] * 3 + [HBM],
            (VMEM,) * (count + 1),
            [pltpu.VMEM((8, LANES), I32), pltpu.SMEM((8, LANES), I32), DMA((count + 1,))],
        )(facts, *tables[4:], a_blocks)
        return sent, place

    def judged(facts, place, rows, tables, after):
        line = jax.ShapeDtypeStruct((1, LANES), I32)
        shapes = (line, line, jax.ShapeDtypeStruct(rows.shape, I32), jax.ShapeDtypeStruct((2,), I32))
        kernel = functools.partial(judge, plan)
        return call(kernel, shapes, [VMEM] * 6, (VMEM, VMEM, VMEM, SMEM))(facts, place, rows, *tables[4:], after)

    def product(J, raw, first, rows, waves, mine, theirs, a_blocks, lefts, start):
        return call(
            functools.partial(multiply, plan, J, raw, len(lefts) // len(plan.others), first),
            result,
            [SMEM, SMEM, VMEM, VMEM] + [HBM] * (2 + len(lefts)),
            HBM,
            [
                pltpu.VMEM((2 * J, bs, bs), F32),
                pltpu.VMEM((nc, bs, bs), F32),
                DMA((2 * J,)),
                DMA((nc,)),
            ],
            input_output_aliases={5 + len(lefts): 0},
        )(rows, waves, mine, theirs, a_blocks, *lefts, start)

    if not plan.whole:
        a_pattern = lax.all_gather(a_pattern, "col", axis=1, tiled=True)
    b0 = plan.rows * plan.W
    entries = jnp.pad(b_pattern, ((0, plan.rows - 1), (b0, LANES - b0 - nc)))
    entries += jnp.pad(c_pattern, ((0, plan.rows - 1), (b0 + nc, LANES - b0 - 2 * nc)))
    entries += jnp.pad(a_pattern, ((0, 0), (0, LANES - plan.W)))

    b_pieces = b_blocks.reshape(nc, G, R, bs)
    width = plan.slots * bs + LANES
    pieces = call(
        functools.partial(prepare, plan),
        jax.ShapeDtypeStruct((G, R, width), F32),
        [VMEM, HBM],
        HBM,
        [
            pltpu.VMEM((plan.slots, G, R, bs), F32),
            pltpu.VMEM((G, R, LANES), F32),
            DMA((plan.slots, 2)),
            DMA((plan.slots + 1, 2)),
        ],
    )(entries, b_pieces)
    got = exchange(pieces)
    lefts = []
    for wave in range(1 if plan.whole else plan.waves):
        staged = call(
            functools.partial(stage, plan, wave),
            (block,) * plan.ndep,
            [VMEM, HBM],
            (VMEM,) * plan.ndep,
            [DMA((plan.rows,))],
        )(entries, a_blocks)
        lefts += shift([staged[dd] for dd, _ in plan.others])

    tables = plan.tables()
    zero = call(
        functools.partial(clear, plan), result, [VMEM], HBM, [pltpu.VMEM((bs, bs), F32), DMA((nc,))]
    )(staged[0])
    got, lefts, zero = lax.optimization_barrier((got, lefts, zero))
    send, rows, facts = listed(J, None, got, [], tables)
    mine = exchange(send)
    sent, place = settled(1, facts, a_blocks, tables)
    waves, waves_again, rows_again, state = judged(facts, place, rows, tables, sent[0] if sent else place)
    sent = shift(sent)
    mine, sent = lax.optimization_barrier((mine, sent))
    lefts = lefts + sent
    theirs = swap(mine)
    near = [pltpu.with_memory_space_constraint(x, pltpu.VMEM) for x in (mine, theirs)]
    c_blocks = product(J, False, True, rows, waves, *near, a_blocks, lefts, zero)

    again = plan.tables(F32)

    def rounds(J, begin, raw, rest, got, state, waves, a_blocks, lefts, c_blocks):
        most = state[1] if plan.whole else lax.pmax(state[1], "col")

        def body(turn, c_blocks):
            send, rows, _ = listed(J, begin + 2 * J * turn, got, rest, again)
            mine = exchange(send)
            return product(J, raw, False, rows, waves, mine, swap(mine), a_blocks, lefts, c_blocks)

        return lax.fori_loop(0, (jnp.maximum(most - begin, 0) + 2 * J - 1) // (2 * J), body, c_blocks)

    def spread_rest(b_pieces):
        return [exchange(b_pieces[plan.slots])] if plan.slots < nc else []

    def done(c_blocks, *_):
        return c_blocks

    def more_rounds(c_blocks, rows, mine, theirs, got, facts, state, waves, a_blocks, b_pieces, *lefts):
        return rounds(plan.more, 2 * J, False, [], got, state, waves, a_blocks, lefts, c_blocks)

    def more_waves(way, c_blocks, rows, mine, theirs, got, facts, state, waves, a_blocks, b_pieces, *lefts):
        sent = settled(2, facts, a_blocks, again)[0]
        for o in range(len(sent)):
            if way in (o, len(sent)):
                sent[o] = shift(sent, [o])[0]
        c_blocks = product(J, False, True, rows, waves, mine, theirs, a_blocks, lefts + tuple(sent), c_blocks)
        return rounds(plan.more, 2 * J, False, [], got, state, waves, a_blocks, lefts + tuple(sent), c_blocks)

    def more_pieces(c_blocks, rows, mine, theirs, got, facts, state, waves, a_blocks, b_pieces, *lefts):
        c_blocks = jnp.zeros_like(c_blocks)
        return rounds(J, 0, False, spread_rest(b_pieces), got, state, waves, a_blocks, lefts, c_blocks)

    def anew(c_blocks, rows, mine, theirs, got, facts, state, waves, a_blocks, b_pieces, *lefts):
        c_blocks = jnp.zeros_like(c_blocks)
        dep = lax.axis_index("depth")
        raw = [lax.dynamic_index_in_dim(a_blocks, (dep + dd) % plan.ndep, keepdims=False) for dd, _ in plan.others]
        return rounds(J, 0, True, spread_rest(b_pieces), got, state, waves, a_blocks, shift(raw), c_blocks)

    index = state[0] if plan.whole else lax.pmax(state[0], "col")
    ways = [functools.partial(more_waves, way) for way in range(len(plan.others) * plan.whole + 1)]
    branches = [done, more_rounds, *ways, more_pieces, anew]
    kept = (rows_again, mine, theirs, got, facts, state, waves_again, a_blocks, b_pieces)
    return lax.switch(index, branches, c_blocks, *kept, *lefts)


def solution(mesh):
    in_specs = (
        P("row", ("depth", "col"), None, None),
        P("row", ("depth", "col")),
        P(("depth", "row"), "col", None, None),
        P(("depth", "row"), "col"),
        P(("row", "depth"), "col"),
    )
    out_specs = P(("row", "depth"), "col", None, None)
    return jax.shard_map(
        functools.partial(local, mesh), mesh=mesh, in_specs=in_specs, out_specs=out_specs, check_vma=False
    )
```
